128 devices in a mesh: rows: 16 (over y, x_lo, core), cols: 8 (over x_hi, z).
Axes of the slice: x: 4 (x_hi: 2, x_lo: 2; x = x_hi * 2 + x_lo), y: 4, z: 4, core: 2. Of those that a mesh axis runs over, the one named last changes fastest.
Arguments:
- tokens: bfloat16 [131072, 1024], P(('rows', 'cols')), may hold values from -40 to 40
- qkv_weight: bfloat16 [1024, 3072], replicated, may hold values from -0.25 to 0.25
- out_weight: bfloat16 [1024, 1024], replicated, may hold values from -0.1875 to 0.1875
- neighbours: int32 [32, 64, 9], P('rows', 'cols'), may hold values from -1 to 2047, as said below
Outputs:
- mixed: bfloat16 [131072, 1024], P(('rows', 'cols'))
The draws below stay inside these ranges and needn't reach their ends.
Inputs may be any that keep to these rules, and one draw needn't show every extreme that they name: `neighbours`: entry k of block (i, j)'s list is the block at offset (k // 3 - 1, k % 3 - 1) from a centre block, or -1 where that block is left out; the centre is (i, j) moved inward just enough to lie one block off every edge of the grid; block (i, j) itself is never left out.
All inputs are finite; a program needn't handle non-finite values.
Results may differ from the reference program's by a relative error of at most 0.014.
Values may be sent and summed in bfloat16 or wider, within the bound.
A program may use at most 192 MiB of HBM per device.

```python
import jax
import jax.numpy as jnp
from jax import lax

D = 1024
HEADS = 16
HEAD_DIM = 64
BLK = 8
NBR = 9
GH = 256
GW = 512
TOKENS = 131072


def draw_tokens(key, part):
    key = jax.random.fold_in(key, 11)
    key_base = jax.random.fold_in(key, 1)
    values = jnp.clip(jax.random.normal(key_base, (TOKENS, D), jnp.float32), -6.0, 6.0)
    return values.astype(jnp.bfloat16)


def draw_qkv_weight(key, part):
    key = jax.random.fold_in(key, 23)
    key_query, key_key, key_value = jax.random.split(key, 3)
    spread = D ** (-0.5)
    query_part = jnp.clip(jax.random.normal(key_query, (D, D), jnp.float32), -6.0, 6.0) * spread
    value_part = jnp.clip(jax.random.normal(key_value, (D, D), jnp.float32), -6.0, 6.0) * spread
    key_part = jnp.clip(jax.random.normal(key_key, (D, D), jnp.float32), -6.0, 6.0) * spread
    return jnp.concatenate([query_part, key_part, value_part], axis=1).astype(jnp.bfloat16)


def draw_neighbours(key, part):
    key = jax.random.fold_in(key, 37)
    block_rows = GH // BLK
    block_cols = GW // BLK
    row_index = jnp.arange(block_rows, dtype=jnp.int32)[:, None, None]
    col_index = jnp.arange(block_cols, dtype=jnp.int32)[None, :, None]
    entry = jnp.arange(NBR, dtype=jnp.int32)[None, None, :]
    centre_row = jnp.clip(row_index, 1, block_rows - 2)
    centre_col = jnp.clip(col_index, 1, block_cols - 2)
    near_row = centre_row + entry // 3 - 1
    near_col = centre_col + entry % 3 - 1
    numbers = near_row * block_cols + near_col
    itself = (near_row == row_index) & (near_col == col_index)
    dropped = jax.random.randint(key, (block_rows, block_cols, NBR), 0, 4) == 0
    return jnp.where(dropped & jnp.logical_not(itself), -1, numbers).astype(jnp.int32)


def gaussian(rng, shape, deviation, limit, kind=jnp.bfloat16):
    return jnp.clip(deviation * jax.random.normal(rng, shape, jnp.float32), -limit, limit).astype(kind)


def setup_inputs(seed: int = 0) -> dict:
    streams_of = jax.random.split(jax.random.key(seed), 5)
    return {
        "tokens": draw_tokens(jax.random.fold_in(streams_of[4], 71), 0),
        "qkv_weight": draw_qkv_weight(jax.random.fold_in(streams_of[4], 71), 0),
        "out_weight": gaussian(streams_of[2], (D, D), D ** -0.5, 0.1875),
        "neighbours": draw_neighbours(jax.random.fold_in(streams_of[4], 71), 0),
    }


def attend_row(query_row, lists, key_blocks):
    block_cols = query_row.shape[0]
    present = lists >= 0
    clamped = jnp.where(present, lists, 0).astype(jnp.int32)
    gathered = key_blocks[clamped].reshape(block_cols, NBR * BLK * BLK, 2 * D)
    key_set = gathered[:, :, :D].astype(jnp.float32).reshape(block_cols, NBR * BLK * BLK, HEADS, HEAD_DIM)
    value_set = gathered[:, :, D:].astype(jnp.float32).reshape(block_cols, NBR * BLK * BLK, HEADS, HEAD_DIM)
    query_set = query_row.astype(jnp.float32).reshape(block_cols, BLK * BLK, HEADS, HEAD_DIM)
    scores = jnp.einsum("bqhd,bkhd->bhqk", query_set, key_set) * (HEAD_DIM ** -0.5)
    key_mask = jnp.repeat(present, BLK * BLK, axis=1)
    scores = jnp.where(key_mask[:, None, None, :], scores, -jnp.inf)
    row_top = jnp.max(scores, axis=-1, keepdims=True)
    weights = jnp.exp(scores - row_top)
    probabilities = (weights / jnp.sum(weights, axis=-1, keepdims=True)).astype(jnp.bfloat16)
    result = jnp.einsum("bhqk,bkhd->bqhd", probabilities.astype(jnp.float32), value_set)
    return result.astype(jnp.bfloat16).reshape(block_cols, BLK * BLK, D)


def reference(tokens, qkv_weight, out_weight, neighbours):
    projected = jnp.dot(tokens, qkv_weight, preferred_element_type=jnp.float32).astype(jnp.bfloat16)
    block_rows = GH // BLK
    block_cols = GW // BLK
    block_data = projected.reshape(block_rows, BLK, block_cols, BLK, 3 * D).transpose(0, 2, 1, 3, 4)
    block_data = block_data.reshape(block_rows * block_cols, BLK * BLK, 3 * D)
    query_rows = block_data[:, :, :D].reshape(block_rows, block_cols, BLK * BLK, D)
    key_blocks = block_data[:, :, D:]
    attended = lax.map(lambda pair: attend_row(pair[0], pair[1], key_blocks), (query_rows, neighbours))
    attended = attended.reshape(block_rows, block_cols, BLK, BLK, D).transpose(0, 2, 1, 3, 4).reshape(TOKENS, D)
    return jnp.dot(attended, out_weight, preferred_element_type=jnp.float32).astype(jnp.bfloat16)
```

```python
import functools

import jax
import jax.numpy as jnp
from jax import lax
from jax.experimental import pallas as pl
from jax.experimental.pallas import tpu as pltpu
from jax.sharding import PartitionSpec as P

MESH = pl.DeviceIdType.MESH
BF16 = jnp.bfloat16
F32 = jnp.float32
D = 1024
HEADS = 16
HEAD_DIM = 64
GROUPS = 64
TILES = 8
SCALE = HEAD_DIM**-0.5
STAGES = ((0, 4, (0, 1)), (4, 2, (2, 3)))
QUAD = 256


def kernel(
    tok, wqkv, wout, nbr, out,
    src, win, keys, vals, quer, att, mix, wqkv_v, wout_v, nb_v, nb_s,
    load_sem, in_send, in_recv, halo_send, halo_recv, nb_send, nb_recv, nb_load, out_send, out_recv,
):
    row, col = lax.axis_index("rows"), lax.axis_index("cols")
    y, x_lo, core = row // 4, (row // 2) % 2, row % 2
    x_hi, z = col // 4, col % 4
    x = 2 * x_hi + x_lo
    g, t = 2 * y + core, 8 * x_lo + col
    has_up, has_down = g > 0, g < TILES - 1

    loads = [pltpu.make_async_copy(tok.at[r], src.at[pl.ds(1, GROUPS), r], load_sem.at[r]) for r in range(2)]
    wload = pltpu.make_async_copy(wqkv, wqkv_v, load_sem.at[2])
    oload = pltpu.make_async_copy(wout, wout_v, load_sem.at[3])
    for load in loads:
        load.start()
    wload.start()
    oload.start()

    barrier = pltpu.get_barrier_semaphore()
    place = 8 * (row % 4) + col

    def greet(i, carry):
        other = (place + i) % 32
        pl.semaphore_signal(barrier, inc=1, device_id=(4 * y + other // 8, other % 8), device_id_type=MESH)
        return carry

    lax.fori_loop(1, 32, greet, 0)
    step_y = 2 * core - 1
    outer = jnp.logical_and(y + step_y >= 0, y + step_y < TILES // 2)

    @pl.when(outer)
    def _():
        pl.semaphore_signal(
            barrier, inc=1, device_id=(4 * (y + step_y) + 2 * x_lo + 1 - core, col), device_id_type=MESH
        )

    src[0] = jnp.zeros((2, 8, D), BF16)
    src[GROUPS + 1] = jnp.zeros((2, 8, D), BF16)

    @pl.when(jnp.logical_not(has_up))
    def _():
        for c in range(6):
            win[c, 0:8] = jnp.zeros((8, 8, D), BF16)

    @pl.when(jnp.logical_not(has_down))
    def _():
        for c in range(6):
            win[c, 40:48] = jnp.zeros((8, 8, D), BF16)

    for load in loads:
        load.wait()
    pl.semaphore_wait(barrier, jnp.where(outer, 32, 31))

    for e in range(2):
        there = 2 * col + e
        dest = (4 * y + 2 * x_hi + x_lo, there % 8)
        own = jnp.logical_and(dest[0] == row, dest[1] == col)

        @pl.when(own)
        def _(dest=dest):
            pltpu.make_async_copy(nbr, nb_v.at[core], nb_recv.at[core]).start()

        @pl.when(jnp.logical_not(own))
        def _(dest=dest, e=e):
            pltpu.make_async_remote_copy(
                nbr, nb_v.at[core], nb_send.at[e], nb_recv.at[core], device_id=dest, device_id_type=MESH
            ).start()

    at_row = 8 + 16 * core + 2 * col
    band = 2 * core + x_hi
    meets = core == x_lo

    for k, (first, count, _) in enumerate(STAGES):

        def send(s, carry, k=k, first=first, count=count):
            turn = (5 * s) % 16
            x2, z2 = (x + turn // 4) % 4, (z + turn) % 4
            col2 = 4 * (x2 // 2) + z2
            t2 = 8 * (x2 % 2) + col2
            source = src.at[pl.ds(4 * t2 + first, count)]
            target = win.at[pl.ds(first, count), pl.ds(at_row, 2)]
            own = jnp.logical_and(s == 0, meets)

            @pl.when(own)
            def _():
                pltpu.make_async_copy(source, target, in_recv.at[k, band]).start()

            @pl.when(jnp.logical_not(own))
            def _():
                pltpu.make_async_remote_copy(
                    source, target, in_send.at[k], in_recv.at[k, band],
                    device_id=(4 * y + 2 * (x2 % 2) + x_lo, col2), device_id_type=MESH,
                ).start()

            return carry

        lax.fori_loop(0, 16, send, 0)

    def band_wait(k, b):
        part = win.at[pl.ds(STAGES[k][0], STAGES[k][1]), pl.ds(8 + 8 * b, 8)]
        pltpu.make_async_copy(part, part, in_recv.at[k, b]).wait()

    def halo(k, down):
        first, count, _ = STAGES[k]
        g2 = g + 1 if down else g - 1
        source = win.at[pl.ds(first, count), pl.ds(32 if down else 8, 8)]
        target = win.at[pl.ds(first, count), pl.ds(0 if down else 40, 8)]
        way = 1 if down else 0
        return pltpu.make_async_remote_copy(
            source, target, halo_send.at[k, way], halo_recv.at[k, way],
            device_id=(4 * (g2 // 2) + 2 * x_lo + g2 % 2, col), device_id_type=MESH,
        )

    def arrive(k):
        band_wait(k, 0)

        @pl.when(has_up)
        def _():
            halo(k, False).start()

        band_wait(k, 3)

        @pl.when(has_down)
        def _():
            halo(k, True).start()

        band_wait(k, 1)
        band_wait(k, 2)

    def halo_wait(k):
        @pl.when(has_up)
        def _():
            halo(k, True).wait_recv()

        @pl.when(has_down)
        def _():
            halo(k, False).wait_recv()

    def project_inner(c):
        x_in = win[c, 8:40].reshape(256, D)

        def tile(n, carry):
            at = pl.multiple_of(n * 512, 512)
            kk = jnp.dot(x_in, wqkv_v[:, pl.ds(D + at, 512)], preferred_element_type=F32)
            keys[c, 64:320, pl.ds(at, 512)] = kk.astype(BF16)
            vv = jnp.dot(x_in, wqkv_v[:, pl.ds(2 * D + at, 512)], preferred_element_type=F32)
            vals[c, 64:320, pl.ds(at, 512)] = vv.astype(BF16)
            return carry

        lax.fori_loop(0, 2, tile, 0)

    def project_queries(j):
        x_in = win[j + 1, 8:40].reshape(256, D)

        def tile(n, carry):
            at = pl.multiple_of(n * 512, 512)
            qq = jnp.dot(x_in, wqkv_v[:, pl.ds(at, 512)], preferred_element_type=F32)
            quer[j, :, pl.ds(at, 512)] = (qq.astype(BF16) * SCALE).astype(BF16)
            return carry

        lax.fori_loop(0, 2, tile, 0)

    def project_halo(first, count):
        parts = []
        for c in range(first, first + count):
            parts += [win[c, 0:8].reshape(64, D), win[c, 40:48].reshape(64, D)]
        x_in = jnp.concatenate(parts, axis=0)

        def tile(n, carry):
            at = pl.multiple_of(n * 512, 512)
            kk = jnp.dot(x_in, wqkv_v[:, pl.ds(D + at, 512)], preferred_element_type=F32).astype(BF16)
            vv = jnp.dot(x_in, wqkv_v[:, pl.ds(2 * D + at, 512)], preferred_element_type=F32).astype(BF16)
            for i, c in enumerate(range(first, first + count)):
                keys[c, 0:64, pl.ds(at, 512)] = kk[128 * i : 128 * i + 64]
                keys[c, 320:384, pl.ds(at, 512)] = kk[128 * i + 64 : 128 * i + 128]
                vals[c, 0:64, pl.ds(at, 512)] = vv[128 * i : 128 * i + 64]
                vals[c, 320:384, pl.ds(at, 512)] = vv[128 * i + 64 : 128 * i + 128]
            return carry

        lax.fori_loop(0, 2, tile, 0)

    lane_head = lax.broadcasted_iota(jnp.int32, (1, QUAD), 1) // HEAD_DIM

    def attend(j):
        at_col = j
        if j == 0:
            at_col = j + jnp.where(t == 0, 1, 0)
        if j == 3:
            at_col = j - jnp.where(t == 15, 1, 0)

        def block(i, carry):
            at_blk = i + jnp.where(jnp.logical_and(g == 0, i == 0), 1, 0)
            at_blk = at_blk - jnp.where(jnp.logical_and(g == TILES - 1, i == 3), 1, 0)
            rows = pl.ds(pl.multiple_of(64 * at_blk, 64), 192)
            q_rows = pl.ds(pl.multiple_of(64 * i, 64), 64)
            key_at = lax.broadcasted_iota(jnp.int32, (1, 576), 1) // 64
            bias = jnp.zeros((1, 576), F32)
            for kc in range(3):
                for kr in range(3):
                    entry = nb_s[i // 2, i % 2, 4 * (col % 2) + j, 3 * kr + kc]
                    here = jnp.where(entry >= 0, 0.0, -jnp.inf).astype(F32)
                    bias = jnp.where(key_at == 3 * kc + kr, here, bias)
            for h in range(HEADS // 4):
                lanes = pl.ds(h * QUAD, QUAD)
                q4 = quer[j, q_rows, lanes]
                stacked = jnp.concatenate(
                    [jnp.where(lane_head == n, q4, jnp.zeros_like(q4)) for n in range(4)], axis=0
                )
                k4 = jnp.concatenate([keys[at_col + kc, rows, lanes] for kc in range(3)], axis=0)
                v4 = jnp.concatenate([vals[at_col + kc, rows, lanes] for kc in range(3)], axis=0)
                s = lax.dot_general(stacked, k4, (((1,), (1,)), ((), ())), preferred_element_type=F32)
                s = s + bias
                p = jnp.exp(s - jnp.max(s, axis=1, keepdims=True))
                total = jnp.sum(p, axis=1, keepdims=True)
                r = jnp.dot(p.astype(BF16), v4, preferred_element_type=F32) / total
                o = jnp.where(lane_head == 0, r[0:64], r[64:128])
                o = jnp.where(lane_head == 2, r[128:192], o)
                o = jnp.where(lane_head == 3, r[192:256], o)
                att[q_rows, lanes] = o.astype(BF16)
            return carry

        lax.fori_loop(0, 4, block, 0)

        def tile(n, carry):
            at = pl.multiple_of(n * 512, 512)
            mm = jnp.dot(att[...], wout_v[:, pl.ds(at, 512)], preferred_element_type=F32).astype(BF16)
            mix[j, :, :, pl.ds(at, 512)] = mm.reshape(32, 8, 512)
            return carry

        lax.fori_loop(0, 2, tile, 0)

    def send_out(k, first, count):
        def send(s, carry):
            turn = (5 * s) % 16
            z2 = (z + turn) % 4
            x_hi2 = (x_hi + turn // 8) % 2
            core2 = (core + turn // 4) % 2
            col2 = 4 * x_hi2 + z2
            pair = 8 * core2 + col2
            source = mix.at[pl.ds(first, count), pl.ds(2 * pair, 2)]
            target = out.at[pl.ds(4 * t + first, count)]
            own = jnp.logical_and(s == 0, meets)

            @pl.when(own)
            def _():
                pltpu.make_async_copy(source, target, out_recv).start()

            @pl.when(jnp.logical_not(own))
            def _():
                pltpu.make_async_remote_copy(
                    source, target, out_send.at[k], out_recv,
                    device_id=(4 * y + 2 * core + core2, col2), device_id_type=MESH,
                ).start()

            return carry

        lax.fori_loop(0, 16, send, 0)

    def lists_in():
        for b in range(2):
            part = nb_v.at[b]
            pltpu.make_async_copy(part, part, nb_recv.at[b]).wait()
        down = pltpu.make_async_copy(nb_v, nb_s, nb_load)
        down.start()
        down.wait()

    wload.wait()
    oload.wait()
    for k, (first, count, columns) in enumerate(STAGES):
        arrive(k)
        for c in range(first, first + count):
            project_inner(c)
            if 1 <= c <= 4:
                project_queries(c - 1)
        halo_wait(k)
        project_halo(first, count)
        if k == 0:
            lists_in()
        for j in columns:
            attend(j)
        send_out(k, columns[0], len(columns))

    for e in range(2):
        there = 2 * col + e
        own = jnp.logical_and(4 * y + 2 * x_hi + x_lo == row, there % 8 == col)

        @pl.when(jnp.logical_not(own))
        def _(e=e):
            pltpu.make_async_copy(nbr, nbr, nb_send.at[e]).wait()

    for k, (first, count, columns) in enumerate(STAGES):
        for number, when in ((15, meets), (16, jnp.logical_not(meets))):

            @pl.when(when)
            def _(k=k, count=count, columns=columns, number=number):
                sent = win.at[pl.ds(0, count), pl.ds(0, 2 * number)]
                pltpu.make_async_copy(sent, sent, in_send.at[k]).wait()
                mixed = mix.at[pl.ds(0, len(columns)), pl.ds(0, 2 * number)]
                pltpu.make_async_copy(mixed, mixed, out_send.at[k]).wait()

        @pl.when(has_up)
        def _(k=k):
            halo(k, False).wait_send()

        @pl.when(has_down)
        def _(k=k):
            halo(k, True).wait_send()

    pltpu.make_async_copy(out, out, out_recv).wait()


def per_device(tokens, qkv_weight, out_weight, neighbours):
    stages = len(STAGES)
    any_space = pl.BlockSpec(memory_space=pl.ANY)
    dma = pltpu.SemaphoreType.DMA
    mixed = pl.pallas_call(
        kernel,
        out_shape=jax.ShapeDtypeStruct((GROUPS, 2, 8, D), BF16),
        in_specs=[any_space] * 4,
        out_specs=any_space,
        scratch_shapes=[
            pltpu.VMEM((GROUPS + 2, 2, 8, D), BF16),
            pltpu.VMEM((6, 48, 8, D), BF16),
            pltpu.VMEM((6, 384, D), BF16),
            pltpu.VMEM((6, 384, D), BF16),
            pltpu.VMEM((4, 256, D), BF16),
            pltpu.VMEM((256, D), BF16),
            pltpu.VMEM((4, 32, 8, D), BF16),
            pltpu.VMEM((D, 3 * D), BF16),
            pltpu.VMEM((D, D), BF16),
            pltpu.VMEM((2, 2, 8, 9), jnp.int32),
            pltpu.SMEM((2, 2, 8, 9), jnp.int32),
            dma((4,)),
            dma((stages,)),
            dma((stages, 4)),
            dma((stages, 2)),
            dma((stages, 2)),
            dma((2,)),
            dma((2,)),
            dma,
            dma((stages,)),
            dma,
        ],
        compiler_params=pltpu.CompilerParams(
            collective_id=0, has_side_effects=True, vmem_limit_bytes=56 * 1024 * 1024
        ),
    )(tokens.reshape(2, GROUPS, 8, D), qkv_weight, out_weight, neighbours)
    return mixed.transpose(1, 0, 2, 3).reshape(1024, D)


def solution(mesh):
    in_specs = (P(("rows", "cols"), None), P(), P(), P("rows", "cols", None))
    out_specs = P(("rows", "cols"), None)
    return jax.shard_map(
        per_device, mesh=mesh, in_specs=in_specs, out_specs=out_specs, check_vma=False
    )
```

```python
import functools

import jax
import jax.numpy as jnp
from jax import lax
from jax.experimental import pallas as pl
from jax.experimental.pallas import tpu as pltpu
from jax.sharding import PartitionSpec as P

MESH = pl.DeviceIdType.MESH
BF16 = jnp.bfloat16
F32 = jnp.float32
D = 1024
HEADS = 16
HEAD_DIM = 64
GROUPS = 64
TILES = 8
SCALE = HEAD_DIM**-0.5
STAGES = 6
COLS = 4
QUAD = 256


def kernel(
    tok, wqkv, wout, nbr, out,
    src, win, keys, vals, quer, att, mix, wqkv_v, wout_v, nb_v, nb_s,
    load_sem, in_send, in_recv, halo_send, halo_recv, nb_send, nb_recv, nb_load, out_send, out_recv,
):
    row, col = lax.axis_index("rows"), lax.axis_index("cols")
    y, x_lo, core = row // 4, (row // 2) % 2, row % 2
    x_hi, z = col // 4, col % 4
    x = 2 * x_hi + x_lo
    g, t = 2 * y + core, 8 * x_lo + col
    has_up, has_down = g > 0, g < TILES - 1

    loads = [pltpu.make_async_copy(tok.at[r], src.at[pl.ds(1, GROUPS), r], load_sem.at[r]) for r in range(2)]
    wload = pltpu.make_async_copy(wqkv, wqkv_v, load_sem.at[2])
    oload = pltpu.make_async_copy(wout, wout_v, load_sem.at[3])
    for load in loads:
        load.start()
    wload.start()
    oload.start()

    barrier = pltpu.get_barrier_semaphore()
    place = 8 * (row % 4) + col

    def greet(i, carry):
        other = (place + i) % 32
        pl.semaphore_signal(barrier, inc=1, device_id=(4 * y + other // 8, other % 8), device_id_type=MESH)
        return carry

    lax.fori_loop(1, 32, greet, 0)
    step_y = 2 * core - 1
    outer = jnp.logical_and(y + step_y >= 0, y + step_y < TILES // 2)

    @pl.when(outer)
    def _():
        pl.semaphore_signal(
            barrier, inc=1, device_id=(4 * (y + step_y) + 2 * x_lo + 1 - core, col), device_id_type=MESH
        )

    src[0] = jnp.zeros((2, 8, D), BF16)
    src[GROUPS + 1] = jnp.zeros((2, 8, D), BF16)

    @pl.when(jnp.logical_not(has_up))
    def _():
        for c in range(6):
            win[c, 0:8] = jnp.zeros((8, 8, D), BF16)

    @pl.when(jnp.logical_not(has_down))
    def _():
        for c in range(6):
            win[c, 40:48] = jnp.zeros((8, 8, D), BF16)

    for load in loads:
        load.wait()
    pl.semaphore_wait(barrier, jnp.where(outer, 32, 31))

    for e in range(2):
        there = 2 * col + e
        dest = (4 * y + 2 * x_hi + x_lo, there % 8)
        own = jnp.logical_and(dest[0] == row, dest[1] == col)

        @pl.when(own)
        def _(dest=dest):
            pltpu.make_async_copy(nbr, nb_v.at[core], nb_recv.at[core]).start()

        @pl.when(jnp.logical_not(own))
        def _(dest=dest, e=e):
            pltpu.make_async_remote_copy(
                nbr, nb_v.at[core], nb_send.at[e], nb_recv.at[core], device_id=dest, device_id_type=MESH
            ).start()

    at_row = 8 + 16 * core + 2 * col
    band = 2 * core + x_hi
    meets = core == x_lo

    shift = jnp.where(t == 0, 1, 0)

    def place_of(k):
        return (k + shift) % 6

    def send_in(n, carry):
        k, s = n // 16, n % 16
        turn = (5 * s) % 16
        x2, z2 = (x + turn // 4) % 4, (z + turn) % 4
        col2 = 4 * (x2 // 2) + z2
        t2 = 8 * (x2 % 2) + col2
        c2 = (k + jnp.where(t2 == 0, 1, 0)) % 6
        source = src.at[4 * t2 + c2]
        target = win.at[c2, pl.ds(at_row, 2)]
        own = jnp.logical_and(s == 0, meets)

        @pl.when(own)
        def _():
            pltpu.make_async_copy(source, target, in_recv.at[k, band]).start()

        @pl.when(jnp.logical_not(own))
        def _():
            pltpu.make_async_remote_copy(
                source, target, in_send, in_recv.at[k, band],
                device_id=(4 * y + 2 * (x2 % 2) + x_lo, col2), device_id_type=MESH,
            ).start()

        return carry

    lax.fori_loop(0, 16 * STAGES, send_in, 0)

    def band_wait(k, b):
        part = win.at[0, pl.ds(8 + 8 * b, 8)]
        pltpu.make_async_copy(part, part, in_recv.at[k, b]).wait()

    def halo(k, down):
        c = place_of(k)
        g2 = g + 1 if down else g - 1
        source = win.at[c, pl.ds(32 if down else 8, 8)]
        target = win.at[c, pl.ds(0 if down else 40, 8)]
        way = 1 if down else 0
        return pltpu.make_async_remote_copy(
            source, target, halo_send.at[k, way], halo_recv.at[k, way],
            device_id=(4 * (g2 // 2) + 2 * x_lo + g2 % 2, col), device_id_type=MESH,
        )

    def arrive(k):
        band_wait(k, 0)

        @pl.when(has_up)
        def _():
            halo(k, False).start()

        band_wait(k, 3)

        @pl.when(has_down)
        def _():
            halo(k, True).start()

        band_wait(k, 1)
        band_wait(k, 2)

    def halo_wait(k):
        @pl.when(has_up)
        def _():
            halo(k, True).wait_recv()

        @pl.when(has_down)
        def _():
            halo(k, False).wait_recv()

    def project(x_in, store):
        def tile(n, carry):
            at = pl.multiple_of(n * 512, 512)
            kk = jnp.dot(x_in, wqkv_v[:, pl.ds(D + at, 512)], preferred_element_type=F32)
            vv = jnp.dot(x_in, wqkv_v[:, pl.ds(2 * D + at, 512)], preferred_element_type=F32)
            store(pl.ds(at, 512), kk.astype(BF16), vv.astype(BF16))
            return carry

        lax.fori_loop(0, 2, tile, 0)

    def project_inner(k):
        c = place_of(k)

        def store(lanes, kk, vv):
            keys[c, 64:320, lanes] = kk
            vals[c, 64:320, lanes] = vv

        project(win[c, 8:40].reshape(256, D), store)

    def project_whole(k):
        c = place_of(k)

        def store(lanes, kk, vv):
            keys[c, :, lanes] = kk
            vals[c, :, lanes] = vv

        project(win[c].reshape(384, D), store)

    def project_halo(ks):
        places = [place_of(k) for k in ks]

        def store(lanes, kk, vv):
            for i, c in enumerate(places):
                keys[c, 0:64, lanes] = kk[128 * i : 128 * i + 64]
                keys[c, 320:384, lanes] = kk[128 * i + 64 : 128 * i + 128]
                vals[c, 0:64, lanes] = vv[128 * i : 128 * i + 64]
                vals[c, 320:384, lanes] = vv[128 * i + 64 : 128 * i + 128]

        parts = []
        for c in places:
            parts += [win[c, 0:8].reshape(64, D), win[c, 40:48].reshape(64, D)]
        project(jnp.concatenate(parts, axis=0), store)

    def project_queries(j):
        x_in = win[j + 1, 8:40].reshape(256, D)

        def tile(n, carry):
            at = pl.multiple_of(n * 512, 512)
            qq = jnp.dot(x_in, wqkv_v[:, pl.ds(at, 512)], preferred_element_type=F32)
            quer[:, pl.ds(at, 512)] = (qq.astype(BF16) * SCALE).astype(BF16)
            return carry

        lax.fori_loop(0, 2, tile, 0)

    lane_head = lax.broadcasted_iota(jnp.int32, (1, QUAD), 1) // HEAD_DIM

    def attend(j, between):
        at_col = j
        if j == 0:
            at_col = j + shift
        if j == 3:
            at_col = j - jnp.where(t == 15, 1, 0)

        def block(i, carry):
            if between is not None:
                pl.when(i == 2)(between)
            at_blk = i + jnp.where(jnp.logical_and(g == 0, i == 0), 1, 0)
            at_blk = at_blk - jnp.where(jnp.logical_and(g == TILES - 1, i == 3), 1, 0)
            rows = pl.ds(pl.multiple_of(64 * at_blk, 64), 192)
            q_rows = pl.ds(pl.multiple_of(64 * i, 64), 64)
            key_at = lax.broadcasted_iota(jnp.int32, (1, 576), 1) // 64
            bias = jnp.zeros((1, 576), F32)
            for kc in range(3):
                for kr in range(3):
                    entry = nb_s[i // 2, i % 2, 4 * (col % 2) + j, 3 * kr + kc]
                    here = jnp.where(entry >= 0, 0.0, -jnp.inf).astype(F32)
                    bias = jnp.where(key_at == 3 * kc + kr, here, bias)
            for h in range(HEADS // 4):
                lanes = pl.ds(h * QUAD, QUAD)
                q4 = quer[q_rows, lanes]
                stacked = jnp.concatenate(
                    [jnp.where(lane_head == n, q4, jnp.zeros_like(q4)) for n in range(4)], axis=0
                )
                k4 = jnp.concatenate([keys[at_col + kc, rows, lanes] for kc in range(3)], axis=0)
                v4 = jnp.concatenate([vals[at_col + kc, rows, lanes] for kc in range(3)], axis=0)
                s = lax.dot_general(stacked, k4, (((1,), (1,)), ((), ())), preferred_element_type=F32)
                s = s + bias
                p = jnp.exp(s - jnp.max(s, axis=1, keepdims=True))
                total = jnp.sum(p, axis=1, keepdims=True)
                r = jnp.dot(p.astype(BF16), v4, preferred_element_type=F32) / total
                o = jnp.where(lane_head == 0, r[0:64], r[64:128])
                o = jnp.where(lane_head == 2, r[128:192], o)
                o = jnp.where(lane_head == 3, r[192:256], o)
                att[q_rows, lanes] = o.astype(BF16)
            return carry

        lax.fori_loop(0, 4, block, 0)

        def tile(n, carry):
            at = pl.multiple_of(n * 512, 512)
            mm = jnp.dot(att[...], wout_v[:, pl.ds(at, 512)], preferred_element_type=F32).astype(BF16)
            mix[j, :, :, pl.ds(at, 512)] = mm.reshape(32, 8, 512)
            return carry

        lax.fori_loop(0, 2, tile, 0)

    def send_out(j):
        def send(s, carry):
            turn = (5 * s) % 16
            z2 = (z + turn) % 4
            x_hi2 = (x_hi + turn // 8) % 2
            core2 = (core + turn // 4) % 2
            col2 = 4 * x_hi2 + z2
            pair = 8 * core2 + col2
            source = mix.at[j, pl.ds(2 * pair, 2)]
            target = out.at[4 * t + j]
            own = jnp.logical_and(s == 0, meets)

            @pl.when(own)
            def _():
                pltpu.make_async_copy(source, target, out_recv).start()

            @pl.when(jnp.logical_not(own))
            def _():
                pltpu.make_async_remote_copy(
                    source, target, out_send, out_recv,
                    device_id=(4 * y + 2 * core + core2, col2), device_id_type=MESH,
                ).start()

            return carry

        lax.fori_loop(0, 16, send, 0)

    def lists_in():
        for b in range(2):
            part = nb_v.at[b]
            pltpu.make_async_copy(part, part, nb_recv.at[b]).wait()
        down = pltpu.make_async_copy(nb_v, nb_s, nb_load)
        down.start()
        down.wait()

    wload.wait()
    oload.wait()
    for k in range(3):
        arrive(k)
        project_inner(k)
    project_queries(0)
    lists_in()
    for k in range(3):
        halo_wait(k)
    project_halo(range(3))
    for j in range(COLS):
        if j > 0:
            project_queries(j)
            halo_wait(j + 2)
            project_whole(j + 2)
        attend(j, functools.partial(arrive, j + 3) if j + 3 < STAGES else None)
        send_out(j)

    for e in range(2):
        there = 2 * col + e
        own = jnp.logical_and(4 * y + 2 * x_hi + x_lo == row, there % 8 == col)

        @pl.when(jnp.logical_not(own))
        def _(e=e):
            pltpu.make_async_copy(nbr, nbr, nb_send.at[e]).wait()

    for number, when in ((15, meets), (16, jnp.logical_not(meets))):

        @pl.when(when)
        def _(number=number):
            sent = win.at[:, pl.ds(0, 2 * number)]
            pltpu.make_async_copy(sent, sent, in_send).wait()
            mixed = mix.at[:, pl.ds(0, 2 * number)]
            pltpu.make_async_copy(mixed, mixed, out_send).wait()

    for k in range(STAGES):

        @pl.when(has_up)
        def _(k=k):
            halo(k, False).wait_send()

        @pl.when(has_down)
        def _(k=k):
            halo(k, True).wait_send()

    pltpu.make_async_copy(out, out, out_recv).wait()


def per_device(tokens, qkv_weight, out_weight, neighbours):
    any_space = pl.BlockSpec(memory_space=pl.ANY)
    dma = pltpu.SemaphoreType.DMA
    mixed = pl.pallas_call(
        kernel,
        out_shape=jax.ShapeDtypeStruct((GROUPS, 2, 8, D), BF16),
        in_specs=[any_space] * 4,
        out_specs=any_space,
        scratch_shapes=[
            pltpu.VMEM((GROUPS + 2, 2, 8, D), BF16),
            pltpu.VMEM((6, 48, 8, D), BF16),
            pltpu.VMEM((6, 384, D), BF16),
            pltpu.VMEM((6, 384, D), BF16),
            pltpu.VMEM((256, D), BF16),
            pltpu.VMEM((256, D), BF16),
            pltpu.VMEM((4, 32, 8, D), BF16),
            pltpu.VMEM((D, 3 * D), BF16),
            pltpu.VMEM((D, D), BF16),
            pltpu.VMEM((2, 2, 8, 9), jnp.int32),
            pltpu.SMEM((2, 2, 8, 9), jnp.int32),
            dma((4,)),
            dma,
            dma((STAGES, 4)),
            dma((STAGES, 2)),
            dma((STAGES, 2)),
            dma((2,)),
            dma((2,)),
            dma,
            dma,
            dma,
        ],
        compiler_params=pltpu.CompilerParams(
            collective_id=0, has_side_effects=True, vmem_limit_bytes=56 * 1024 * 1024
        ),
    )(tokens.reshape(2, GROUPS, 8, D), qkv_weight, out_weight, neighbours)
    return mixed.transpose(1, 0, 2, 3).reshape(1024, D)


def solution(mesh):
    in_specs = (P(("rows", "cols"), None), P(), P(), P("rows", "cols", None))
    out_specs = P(("rows", "cols"), None)
    return jax.shard_map(
        per_device, mesh=mesh, in_specs=in_specs, out_specs=out_specs, check_vma=False
    )
```

```python
import functools

import jax
import jax.numpy as jnp
from jax import lax
from jax.experimental import pallas as pl
from jax.experimental.pallas import tpu as pltpu
from jax.sharding import PartitionSpec as P

MESH = pl.DeviceIdType.MESH
BF16 = jnp.bfloat16
F32 = jnp.float32
D = 1024
HEADS = 16
HEAD_DIM = 64
GROUPS = 64
TILES = 8
SCALE = HEAD_DIM**-0.5
STAGES = 6
COLS = 4
QUAD = 256
QUADS = HEADS // 4
KEYS = 576
MIX = 16


def kernel(
    tok, wqkv, nbr, out,
    src, win, keys, vals, quer, att, wqkv_v, nb_v, nb_s,
    score_a, score_b, prob_a, prob_b, share_a, share_b,
    load_sem, in_send, in_recv, halo_send, halo_recv, nb_send, nb_recv, nb_load, out_send, out_recv,
):
    scores, probs, shares = (score_a, score_b), (prob_a, prob_b), (share_a, share_b)
    row, col = lax.axis_index("rows"), lax.axis_index("cols")
    y, x_lo, core = row // 4, (row // 2) % 2, row % 2
    x_hi, z = col // 4, col % 4
    x = 2 * x_hi + x_lo
    g, t = 2 * y + core, 8 * x_lo + col
    has_up, has_down = g > 0, g < TILES - 1

    loads = [pltpu.make_async_copy(tok.at[r], src.at[pl.ds(1, GROUPS), r], load_sem.at[r]) for r in range(2)]
    wload = pltpu.make_async_copy(wqkv, wqkv_v, load_sem.at[2])
    for load in loads:
        load.start()
    wload.start()

    barrier = pltpu.get_barrier_semaphore()
    place = 8 * (row % 4) + col

    def greet(i, carry):
        other = (place + i) % 32
        pl.semaphore_signal(barrier, inc=1, device_id=(4 * y + other // 8, other % 8), device_id_type=MESH)
        return carry

    lax.fori_loop(1, 32, greet, 0)
    step_y = 2 * core - 1
    outer = jnp.logical_and(y + step_y >= 0, y + step_y < TILES // 2)

    @pl.when(outer)
    def _():
        pl.semaphore_signal(
            barrier, inc=1, device_id=(4 * (y + step_y) + 2 * x_lo + 1 - core, col), device_id_type=MESH
        )

    prob_b[...] = jnp.zeros_like(prob_b)
    share_b[...] = jnp.zeros_like(share_b)
    src[0] = jnp.zeros((2, 8, D), BF16)
    src[GROUPS + 1] = jnp.zeros((2, 8, D), BF16)

    @pl.when(jnp.logical_not(has_up))
    def _():
        for c in range(6):
            win[c, 0:8] = jnp.zeros((8, 8, D), BF16)

    @pl.when(jnp.logical_not(has_down))
    def _():
        for c in range(6):
            win[c, 40:48] = jnp.zeros((8, 8, D), BF16)

    for load in loads:
        load.wait()
    pl.semaphore_wait(barrier, jnp.where(outer, 32, 31))

    for e in range(2):
        there = 2 * col + e
        dest = (4 * y + 2 * x_hi + x_lo, there % 8)
        own = jnp.logical_and(dest[0] == row, dest[1] == col)

        @pl.when(own)
        def _(dest=dest):
            pltpu.make_async_copy(nbr, nb_v.at[core], nb_recv.at[core]).start()

        @pl.when(jnp.logical_not(own))
        def _(dest=dest, e=e):
            pltpu.make_async_remote_copy(
                nbr, nb_v.at[core], nb_send.at[e], nb_recv.at[core], device_id=dest, device_id_type=MESH
            ).start()

    at_row = 8 + 16 * core + 2 * col
    band = 2 * core + x_hi
    meets = core == x_lo

    shift = jnp.where(t == 0, 1, 0)

    def place_of(k):
        return (k + shift) % 6

    def send_in(n, carry):
        k, s = n // 16, n % 16
        turn = (5 * s) % 16
        x2, z2 = (x + turn // 4) % 4, (z + turn) % 4
        col2 = 4 * (x2 // 2) + z2
        t2 = 8 * (x2 % 2) + col2
        c2 = (k + jnp.where(t2 == 0, 1, 0)) % 6
        source = src.at[4 * t2 + c2]
        target = win.at[c2, pl.ds(at_row, 2)]
        own = jnp.logical_and(s == 0, meets)

        @pl.when(own)
        def _():
            pltpu.make_async_copy(source, target, in_recv.at[k, band]).start()

        @pl.when(jnp.logical_not(own))
        def _():
            pltpu.make_async_remote_copy(
                source, target, in_send, in_recv.at[k, band],
                device_id=(4 * y + 2 * (x2 % 2) + x_lo, col2), device_id_type=MESH,
            ).start()

        return carry

    lax.fori_loop(0, 16 * STAGES, send_in, 0)

    def band_wait(k, b):
        part = win.at[0, pl.ds(8 + 8 * b, 8)]
        pltpu.make_async_copy(part, part, in_recv.at[k, b]).wait()

    def halo(k, down):
        c = place_of(k)
        g2 = g + 1 if down else g - 1
        source = win.at[c, pl.ds(32 if down else 8, 8)]
        target = win.at[c, pl.ds(0 if down else 40, 8)]
        way = 1 if down else 0
        return pltpu.make_async_remote_copy(
            source, target, halo_send.at[k, way], halo_recv.at[k, way],
            device_id=(4 * (g2 // 2) + 2 * x_lo + g2 % 2, col), device_id_type=MESH,
        )

    def arrive(k):
        band_wait(k, 0)

        @pl.when(has_up)
        def _():
            halo(k, False).start()

        band_wait(k, 3)

        @pl.when(has_down)
        def _():
            halo(k, True).start()

        band_wait(k, 1)
        band_wait(k, 2)

    def halo_wait(k):
        @pl.when(has_up)
        def _():
            halo(k, True).wait_recv()

        @pl.when(has_down)
        def _():
            halo(k, False).wait_recv()

    def project(x_in, store):
        def tile(n, carry):
            at = pl.multiple_of(n * 512, 512)
            kk = jnp.dot(x_in, wqkv_v[:, pl.ds(D + at, 512)], preferred_element_type=F32)
            vv = jnp.dot(x_in, wqkv_v[:, pl.ds(2 * D + at, 512)], preferred_element_type=F32)
            store(pl.ds(at, 512), kk.astype(BF16), vv.astype(BF16))
            return carry

        lax.fori_loop(0, 2, tile, 0)

    def project_inner(k):
        c = place_of(k)

        def store(lanes, kk, vv):
            keys[c, 64:320, lanes] = kk
            vals[c, 64:320, lanes] = vv

        project(win[c, 8:40].reshape(256, D), store)

    def project_whole(k):
        c = place_of(k)

        def store(lanes, kk, vv):
            keys[c, :, lanes] = kk
            vals[c, :, lanes] = vv

        project(win[c].reshape(384, D), store)

    def project_halo(ks):
        places = [place_of(k) for k in ks]

        def store(lanes, kk, vv):
            for i, c in enumerate(places):
                keys[c, 0:64, lanes] = kk[128 * i : 128 * i + 64]
                keys[c, 320:384, lanes] = kk[128 * i + 64 : 128 * i + 128]
                vals[c, 0:64, lanes] = vv[128 * i : 128 * i + 64]
                vals[c, 320:384, lanes] = vv[128 * i + 64 : 128 * i + 128]

        parts = []
        for c in places:
            parts += [win[c, 0:8].reshape(64, D), win[c, 40:48].reshape(64, D)]
        project(jnp.concatenate(parts, axis=0), store)

    def project_queries(j):
        x_in = win[j + 1, 8:40].reshape(256, D)

        def tile(n, carry):
            at = pl.multiple_of(n * 512, 512)
            qq = jnp.dot(x_in, wqkv_v[:, pl.ds(at, 512)], preferred_element_type=F32)
            quer[j, :, pl.ds(at, 512)] = (qq.astype(BF16) * SCALE).astype(BF16)
            return carry

        lax.fori_loop(0, 2, tile, 0)

    lane_head = lax.broadcasted_iota(jnp.int32, (1, QUAD), 1) // HEAD_DIM

    key_at = lax.broadcasted_iota(jnp.int32, (1, KEYS), 1) // 64

    def attend(j, between):
        at_col = j
        if j == 0:
            at_col = j + shift
        if j == 3:
            at_col = j - jnp.where(t == 15, 1, 0)

        def key_rows(i):
            at_blk = i + jnp.where(jnp.logical_and(g == 0, i == 0), 1, 0)
            at_blk = at_blk - jnp.where(jnp.logical_and(g == TILES - 1, i == 3), 1, 0)
            return pl.ds(pl.multiple_of(64 * at_blk, 64), 192)

        def score(i, h):
            rows, lanes = key_rows(i), pl.ds(h * QUAD, QUAD)
            q4 = quer[j, pl.ds(pl.multiple_of(64 * i, 64), 64), lanes]
            stacked = jnp.concatenate(
                [jnp.where(lane_head == n, q4, jnp.zeros_like(q4)) for n in range(4)], axis=0
            )
            k4 = jnp.concatenate([keys[at_col + kc, rows, lanes] for kc in range(3)], axis=0)
            scores[h % 2][...] = lax.dot_general(
                stacked, k4, (((1,), (1,)), ((), ())), preferred_element_type=F32
            )

        def soften(bias, h):
            for r in range(0, QUAD, 32):
                s = scores[h % 2][r : r + 32, :] + bias
                p = jnp.exp(s - jnp.max(s, axis=1, keepdims=True))
                probs[h % 2][r : r + 32, :] = p.astype(BF16)
                share = 1.0 / jnp.sum(p, axis=1, keepdims=True)
                shares[h % 2][r : r + 32, :] = jnp.broadcast_to(share, (32, 128))

        def gather(i, h):
            rows, lanes = key_rows(i), pl.ds(h * QUAD, QUAD)
            v4 = jnp.concatenate([vals[at_col + kc, rows, lanes] for kc in range(3)], axis=0)
            r = jnp.dot(probs[h % 2][...], v4, preferred_element_type=F32)
            share = shares[h % 2][...]
            r = r * jnp.concatenate([share, share], axis=1)
            o = jnp.where(lane_head == 0, r[0:64], r[64:128])
            o = jnp.where(lane_head == 2, r[128:192], o)
            o = jnp.where(lane_head == 3, r[192:256], o)
            att[j, pl.ds(pl.multiple_of(64 * i, 64), 64), lanes] = o.astype(BF16)

        def block(n, carry):
            if between is not None:
                pl.when(n == 2)(between)
            i, before, after = turned(n), turned(jnp.maximum(n - 1, 0)), turned(jnp.minimum(n + 1, 3))
            bias = jnp.zeros((1, KEYS), F32)
            for kc in range(3):
                for kr in range(3):
                    entry = nb_s[i // 2, i % 2, 4 * (col % 2) + j, 3 * kr + kc]
                    here = jnp.where(entry >= 0, 0.0, -jnp.inf).astype(F32)
                    bias = jnp.where(key_at == 3 * kc + kr, here, bias)
            for h in range(QUADS):
                if h < QUADS - 1:
                    score(i, h + 1)
                else:
                    score(after, 0)
                if h > 0:
                    gather(i, h - 1)
                else:
                    gather(before, QUADS - 1)
                soften(bias, h)

            @pl.when(n > 0)
            def _():
                send_out(j, before)

            return carry

        score(turned(0), 0)
        lax.fori_loop(0, 4, block, 0)
        gather(turned(3), QUADS - 1)
        send_out(j, turned(3))

    def turned(n):
        return (n + 2 * core + x_hi) % 4

    def send_out(j, i):
        def send(s, carry):
            z2 = (z + s) % 4
            source = att.at[j, pl.ds(pl.multiple_of(64 * i + 16 * z2, 16), 16)]
            target = out.at[4 * t + j]
            own = jnp.logical_and(jnp.logical_and(s == 0, meets), i == 2 * core + x_hi)

            @pl.when(own)
            def _():
                pltpu.make_async_copy(source, target, out_recv).start()

            @pl.when(jnp.logical_not(own))
            def _():
                pltpu.make_async_remote_copy(
                    source, target, out_send, out_recv,
                    device_id=(4 * y + 2 * core + i // 2, 4 * (i % 2) + z2), device_id_type=MESH,
                ).start()

            return carry

        lax.fori_loop(0, 4, send, 0)

    def lists_in():
        for b in range(2):
            part = nb_v.at[b]
            pltpu.make_async_copy(part, part, nb_recv.at[b]).wait()
        down = pltpu.make_async_copy(nb_v, nb_s, nb_load)
        down.start()
        down.wait()

    wload.wait()
    arrive(0)
    project_inner(0)
    arrive(1)
    project_inner(1)
    project_queries(0)
    halo_wait(0)
    project_halo((0,))
    lists_in()
    arrive(2)
    project_inner(2)
    project_queries(1)
    halo_wait(1)
    halo_wait(2)
    project_halo((1, 2))
    for j in range(COLS):
        if j > 0:
            if j > 1:
                project_queries(j)
            halo_wait(j + 2)
            project_whole(j + 2)
        attend(j, functools.partial(arrive, j + 3) if j + 3 < STAGES else None)

    for e in range(2):
        there = 2 * col + e
        own = jnp.logical_and(4 * y + 2 * x_hi + x_lo == row, there % 8 == col)

        @pl.when(jnp.logical_not(own))
        def _(e=e):
            pltpu.make_async_copy(nbr, nbr, nb_send.at[e]).wait()

    for number, when in ((15, meets), (16, jnp.logical_not(meets))):

        @pl.when(when)
        def _(number=number):
            sent = win.at[:, pl.ds(0, 2 * number)]
            pltpu.make_async_copy(sent, sent, in_send).wait()
            back = att.at[:, pl.ds(0, 16 * number)]
            pltpu.make_async_copy(back, back, out_send).wait()

    for k in range(STAGES):

        @pl.when(has_up)
        def _(k=k):
            halo(k, False).wait_send()

        @pl.when(has_down)
        def _(k=k):
            halo(k, True).wait_send()

    pltpu.make_async_copy(out, out, out_recv).wait()


def mix_kernel(att, wout, out):
    mm = jnp.dot(att[...].reshape(16 * MIX, D), wout[...], preferred_element_type=F32).astype(BF16)
    mm = mm.reshape(MIX, 2, 8, D)
    for r in range(2):
        out[r] = mm[:, r]


def per_device(tokens, qkv_weight, out_weight, neighbours):
    any_space = pl.BlockSpec(memory_space=pl.ANY)
    dma = pltpu.SemaphoreType.DMA
    attended = pl.pallas_call(
        kernel,
        out_shape=jax.ShapeDtypeStruct((GROUPS, 16, D), BF16),
        in_specs=[any_space] * 3,
        out_specs=any_space,
        scratch_shapes=[
            pltpu.VMEM((GROUPS + 2, 2, 8, D), BF16),
            pltpu.VMEM((6, 48, 8, D), BF16),
            pltpu.VMEM((6, 384, D), BF16),
            pltpu.VMEM((6, 384, D), BF16),
            pltpu.VMEM((4, 256, D), BF16),
            pltpu.VMEM((4, 256, D), BF16),
            pltpu.VMEM((D, 3 * D), BF16),
            pltpu.VMEM((2, 2, 8, 9), jnp.int32),
            pltpu.SMEM((2, 2, 8, 9), jnp.int32),
            pltpu.VMEM((QUAD, KEYS), F32),
            pltpu.VMEM((QUAD, KEYS), F32),
            pltpu.VMEM((QUAD, KEYS), BF16),
            pltpu.VMEM((QUAD, KEYS), BF16),
            pltpu.VMEM((QUAD, 128), F32),
            pltpu.VMEM((QUAD, 128), F32),
            dma((3,)),
            dma,
            dma((STAGES, 4)),
            dma((STAGES, 2)),
            dma((STAGES, 2)),
            dma((2,)),
            dma((2,)),
            dma,
            dma,
            dma,
        ],
        compiler_params=pltpu.CompilerParams(
            collective_id=0, has_side_effects=True, vmem_limit_bytes=56 * 1024 * 1024
        ),
    )(tokens.reshape(2, GROUPS, 8, D), qkv_weight, neighbours)
    mixed = pl.pallas_call(
        mix_kernel,
        out_shape=jax.ShapeDtypeStruct((2, GROUPS, 8, D), BF16),
        grid=(GROUPS // MIX,),
        in_specs=[
            pl.BlockSpec((MIX, 16, D), lambda n: (n, 0, 0)),
            pl.BlockSpec((D, D), lambda n: (0, 0)),
        ],
        out_specs=pl.BlockSpec((2, MIX, 8, D), lambda n: (0, n, 0, 0)),
        compiler_params=pltpu.CompilerParams(vmem_limit_bytes=32 * 1024 * 1024),
    )(attended, out_weight)
    return mixed.reshape(1024, D)


def solution(mesh):
    in_specs = (P(("rows", "cols"), None), P(), P(), P("rows", "cols", None))
    out_specs = P(("rows", "cols"), None)
    return jax.shard_map(
        per_device, mesh=mesh, in_specs=in_specs, out_specs=out_specs, check_vma=False
    )
```

```python
import functools

import jax
import jax.numpy as jnp
from jax import lax
from jax.experimental import pallas as pl
from jax.experimental.pallas import tpu as pltpu
from jax.sharding import PartitionSpec as P

MESH = pl.DeviceIdType.MESH
BF16 = jnp.bfloat16
F32 = jnp.float32
D = 1024
HEADS = 16
HEAD_DIM = 64
GROUPS = 64
TILES = 8
SCALE = HEAD_DIM**-0.5
STAGES = 6
COLS = 4
QUAD = 256
QUADS = HEADS // 4
KEYS = 576
MIX = 16


def kernel(
    tok, wqkv, nbr, out,
    src, win, keys, vals, quer, att, wqkv_v, nb_v, nb_s,
    score_a, score_b, prob_a, prob_b, share_a, share_b,
    load_sem, in_send, in_recv, halo_send, halo_recv, nb_send, nb_recv, nb_load, out_send, out_recv,
):
    scores, probs, shares = (score_a, score_b), (prob_a, prob_b), (share_a, share_b)
    row, col = lax.axis_index("rows"), lax.axis_index("cols")
    y, x_lo, core = row // 4, (row // 2) % 2, row % 2
    x_hi, z = col // 4, col % 4
    x = 2 * x_hi + x_lo
    g, t = 2 * y + core, 8 * x_lo + col
    has_up, has_down = g > 0, g < TILES - 1

    loads = [pltpu.make_async_copy(tok.at[r], src.at[pl.ds(1, GROUPS), r], load_sem.at[r]) for r in range(2)]
    wload = pltpu.make_async_copy(wqkv, wqkv_v, load_sem.at[2])
    for load in loads:
        load.start()
    wload.start()

    barrier = pltpu.get_barrier_semaphore()
    place = 8 * (row % 4) + col

    def greet(i, carry):
        other = (place + i) % 32
        pl.semaphore_signal(barrier, inc=1, device_id=(4 * y + other // 8, other % 8), device_id_type=MESH)
        return carry

    lax.fori_loop(1, 32, greet, 0)
    step_y = 2 * core - 1
    outer = jnp.logical_and(y + step_y >= 0, y + step_y < TILES // 2)

    @pl.when(outer)
    def _():
        pl.semaphore_signal(
            barrier, inc=1, device_id=(4 * (y + step_y) + 2 * x_lo + 1 - core, col), device_id_type=MESH
        )

    prob_b[...] = jnp.zeros_like(prob_b)
    share_b[...] = jnp.zeros_like(share_b)
    src[0] = jnp.zeros((2, 8, D), BF16)
    src[GROUPS + 1] = jnp.zeros((2, 8, D), BF16)

    @pl.when(jnp.logical_not(has_up))
    def _():
        for c in range(6):
            win[c, 0:8] = jnp.zeros((8, 8, D), BF16)

    @pl.when(jnp.logical_not(has_down))
    def _():
        for c in range(6):
            win[c, 40:48] = jnp.zeros((8, 8, D), BF16)

    for load in loads:
        load.wait()
    pl.semaphore_wait(barrier, jnp.where(outer, 32, 31))

    for e in range(2):
        there = 2 * col + e
        dest = (4 * y + 2 * x_hi + x_lo, there % 8)
        own = jnp.logical_and(dest[0] == row, dest[1] == col)

        @pl.when(own)
        def _(dest=dest):
            pltpu.make_async_copy(nbr, nb_v.at[core], nb_recv.at[core]).start()

        @pl.when(jnp.logical_not(own))
        def _(dest=dest, e=e):
            pltpu.make_async_remote_copy(
                nbr, nb_v.at[core], nb_send.at[e], nb_recv.at[core], device_id=dest, device_id_type=MESH
            ).start()

    at_row = 8 + 16 * core + 2 * col
    band = 2 * core + x_hi
    meets = core == x_lo

    shift = jnp.where(t == 0, 1, 0)

    def place_of(k):
        return (k + shift) % 6

    def send_in(n, carry):
        k, s = n // 16, n % 16
        turn = (5 * s) % 16
        x2, z2 = (x + turn // 4) % 4, (z + turn) % 4
        col2 = 4 * (x2 // 2) + z2
        t2 = 8 * (x2 % 2) + col2
        c2 = (k + jnp.where(t2 == 0, 1, 0)) % 6
        source = src.at[4 * t2 + c2]
        target = win.at[c2, pl.ds(at_row, 2)]
        own = jnp.logical_and(s == 0, meets)

        @pl.when(own)
        def _():
            pltpu.make_async_copy(source, target, in_recv.at[k, band]).start()

        @pl.when(jnp.logical_not(own))
        def _():
            pltpu.make_async_remote_copy(
                source, target, in_send, in_recv.at[k, band],
                device_id=(4 * y + 2 * (x2 % 2) + x_lo, col2), device_id_type=MESH,
            ).start()

        return carry

    lax.fori_loop(0, 16 * STAGES, send_in, 0)

    def band_wait(k, b):
        part = win.at[0, pl.ds(8 + 8 * b, 8)]
        pltpu.make_async_copy(part, part, in_recv.at[k, b]).wait()

    def halo(k, down):
        c = place_of(k)
        g2 = g + 1 if down else g - 1
        source = win.at[c, pl.ds(32 if down else 8, 8)]
        target = win.at[c, pl.ds(0 if down else 40, 8)]
        way = 1 if down else 0
        return pltpu.make_async_remote_copy(
            source, target, halo_send.at[k, way], halo_recv.at[k, way],
            device_id=(4 * (g2 // 2) + 2 * x_lo + g2 % 2, col), device_id_type=MESH,
        )

    def arrive(k):
        band_wait(k, 0)

        @pl.when(has_up)
        def _():
            halo(k, False).start()

        band_wait(k, 3)

        @pl.when(has_down)
        def _():
            halo(k, True).start()

        band_wait(k, 1)
        band_wait(k, 2)

    def halo_wait(k):
        @pl.when(has_up)
        def _():
            halo(k, True).wait_recv()

        @pl.when(has_down)
        def _():
            halo(k, False).wait_recv()

    def project(x_in, store):
        kk = jnp.dot(x_in, wqkv_v[:, D : 2 * D], preferred_element_type=F32)
        vv = jnp.dot(x_in, wqkv_v[:, 2 * D :], preferred_element_type=F32)
        store(slice(None), kk.astype(BF16), vv.astype(BF16))

    def project_inner(k):
        c = place_of(k)

        def store(lanes, kk, vv):
            keys[c, 64:320, lanes] = kk
            vals[c, 64:320, lanes] = vv

        project(win[c, 8:40].reshape(256, D), store)

    def project_whole(k):
        c = place_of(k)

        def store(lanes, kk, vv):
            keys[c, :, lanes] = kk
            vals[c, :, lanes] = vv

        project(win[c].reshape(384, D), store)

    def project_halo(ks):
        places = [place_of(k) for k in ks]

        def store(lanes, kk, vv):
            for i, c in enumerate(places):
                keys[c, 0:64, lanes] = kk[128 * i : 128 * i + 64]
                keys[c, 320:384, lanes] = kk[128 * i + 64 : 128 * i + 128]
                vals[c, 0:64, lanes] = vv[128 * i : 128 * i + 64]
                vals[c, 320:384, lanes] = vv[128 * i + 64 : 128 * i + 128]

        parts = []
        for c in places:
            parts += [win[c, 0:8].reshape(64, D), win[c, 40:48].reshape(64, D)]
        project(jnp.concatenate(parts, axis=0), store)

    def project_queries(j):
        x_in = win[j + 1, 8:40].reshape(256, D)

        qq = jnp.dot(x_in, wqkv_v[:, :D], preferred_element_type=F32)
        quer[j] = (qq.astype(BF16) * SCALE).astype(BF16)

    lane_head = lax.broadcasted_iota(jnp.int32, (1, QUAD), 1) // HEAD_DIM

    key_at = lax.broadcasted_iota(jnp.int32, (1, KEYS), 1) // 64

    def attend(j, between):
        at_col = j
        if j == 0:
            at_col = j + shift
        if j == 3:
            at_col = j - jnp.where(t == 15, 1, 0)

        def key_rows(i):
            at_blk = i + jnp.where(jnp.logical_and(g == 0, i == 0), 1, 0)
            at_blk = at_blk - jnp.where(jnp.logical_and(g == TILES - 1, i == 3), 1, 0)
            return pl.ds(pl.multiple_of(64 * at_blk, 64), 192)

        def score(i, h):
            rows, lanes = key_rows(i), pl.ds(h * QUAD, QUAD)
            q4 = quer[j, pl.ds(pl.multiple_of(64 * i, 64), 64), lanes]
            stacked = jnp.concatenate(
                [jnp.where(lane_head == n, q4, jnp.zeros_like(q4)) for n in range(4)], axis=0
            )
            k4 = jnp.concatenate([keys[at_col + kc, rows, lanes] for kc in range(3)], axis=0)
            scores[h % 2][...] = lax.dot_general(
                stacked, k4, (((1,), (1,)), ((), ())), preferred_element_type=F32
            )

        def soften(bias, h):
            for r in range(0, QUAD, 32):
                s = scores[h % 2][r : r + 32, :] + bias
                p = jnp.exp(s - jnp.max(s, axis=1, keepdims=True))
                probs[h % 2][r : r + 32, :] = p.astype(BF16)
                share = 1.0 / jnp.sum(p, axis=1, keepdims=True)
                shares[h % 2][r : r + 32, :] = jnp.broadcast_to(share, (32, 128))

        def gather(i, h):
            rows, lanes = key_rows(i), pl.ds(h * QUAD, QUAD)
            v4 = jnp.concatenate([vals[at_col + kc, rows, lanes] for kc in range(3)], axis=0)
            r = jnp.dot(probs[h % 2][...], v4, preferred_element_type=F32)
            share = shares[h % 2][...]
            r = r * jnp.concatenate([share, share], axis=1)
            o = jnp.where(lane_head == 0, r[0:64], r[64:128])
            o = jnp.where(lane_head == 2, r[128:192], o)
            o = jnp.where(lane_head == 3, r[192:256], o)
            att[j, pl.ds(pl.multiple_of(64 * i, 64), 64), lanes] = o.astype(BF16)

        def block(n, carry):
            if between is not None:
                pl.when(n == 2)(between)
            i, before, after = turned(n), turned(jnp.maximum(n - 1, 0)), turned(jnp.minimum(n + 1, 3))
            bias = jnp.zeros((1, KEYS), F32)
            for kc in range(3):
                for kr in range(3):
                    entry = nb_s[i // 2, i % 2, 4 * (col % 2) + j, 3 * kr + kc]
                    here = jnp.where(entry >= 0, 0.0, -jnp.inf).astype(F32)
                    bias = jnp.where(key_at == 3 * kc + kr, here, bias)
            for h in range(QUADS):
                if h < QUADS - 1:
                    score(i, h + 1)
                else:
                    score(after, 0)
                if h > 0:
                    gather(i, h - 1)
                else:
                    gather(before, QUADS - 1)
                soften(bias, h)

            @pl.when(n > 0)
            def _():
                send_out(j, before)

            return carry

        score(turned(0), 0)
        lax.fori_loop(0, 4, block, 0)
        gather(turned(3), QUADS - 1)
        send_out(j, turned(3))

    def turned(n):
        return (n + 2 * core + x_hi) % 4

    def send_out(j, i):
        def send(s, carry):
            z2 = (z + s) % 4
            source = att.at[j, pl.ds(pl.multiple_of(64 * i + 16 * z2, 16), 16)]
            target = out.at[4 * t + j]
            own = jnp.logical_and(jnp.logical_and(s == 0, meets), i == 2 * core + x_hi)

            @pl.when(own)
            def _():
                pltpu.make_async_copy(source, target, out_recv).start()

            @pl.when(jnp.logical_not(own))
            def _():
                pltpu.make_async_remote_copy(
                    source, target, out_send, out_recv,
                    device_id=(4 * y + 2 * core + i // 2, 4 * (i % 2) + z2), device_id_type=MESH,
                ).start()

            return carry

        lax.fori_loop(0, 4, send, 0)

    def lists_in():
        for b in range(2):
            part = nb_v.at[b]
            pltpu.make_async_copy(part, part, nb_recv.at[b]).wait()
        down = pltpu.make_async_copy(nb_v, nb_s, nb_load)
        down.start()
        down.wait()

    wload.wait()
    arrive(0)
    project_inner(0)
    arrive(1)
    project_inner(1)
    project_queries(0)
    halo_wait(0)
    project_halo((0,))
    lists_in()
    arrive(2)
    project_inner(2)
    project_queries(1)
    halo_wait(1)
    halo_wait(2)
    project_halo((1, 2))
    for j in range(COLS):
        if j > 0:
            if j > 1:
                project_queries(j)
            halo_wait(j + 2)
            project_whole(j + 2)
        attend(j, functools.partial(arrive, j + 3) if j + 3 < STAGES else None)

    for e in range(2):
        there = 2 * col + e
        own = jnp.logical_and(4 * y + 2 * x_hi + x_lo == row, there % 8 == col)

        @pl.when(jnp.logical_not(own))
        def _(e=e):
            pltpu.make_async_copy(nbr, nbr, nb_send.at[e]).wait()

    for number, when in ((15, meets), (16, jnp.logical_not(meets))):

        @pl.when(when)
        def _(number=number):
            sent = win.at[:, pl.ds(0, 2 * number)]
            pltpu.make_async_copy(sent, sent, in_send).wait()
            back = att.at[:, pl.ds(0, 16 * number)]
            pltpu.make_async_copy(back, back, out_send).wait()

    for k in range(STAGES):

        @pl.when(has_up)
        def _(k=k):
            halo(k, False).wait_send()

        @pl.when(has_down)
        def _(k=k):
            halo(k, True).wait_send()

    pltpu.make_async_copy(out, out, out_recv).wait()


def mix_kernel(att, wout, out, mixed, out_sem):
    parts = GROUPS // MIX
    at = lambda n: pl.ds(n * MIX, MIX)
    stores = [pltpu.make_async_copy(mixed.at[n], out.at[:, at(n)], out_sem.at[n]) for n in range(parts)]
    for n in range(parts):
        x_in = att[at(n)].reshape(16 * MIX, D)
        mm = jnp.dot(x_in, wout[...], preferred_element_type=F32).astype(BF16)
        mm = mm.reshape(MIX, 2, 8, D)
        for r in range(2):
            mixed[n, r] = mm[:, r]
        stores[n].start()
    for store in stores:
        store.wait()


def per_device(tokens, qkv_weight, out_weight, neighbours):
    any_space = pl.BlockSpec(memory_space=pl.ANY)
    dma = pltpu.SemaphoreType.DMA
    attended = pl.pallas_call(
        kernel,
        out_shape=jax.ShapeDtypeStruct((GROUPS, 16, D), BF16),
        in_specs=[any_space] * 3,
        out_specs=any_space,
        scratch_shapes=[
            pltpu.VMEM((GROUPS + 2, 2, 8, D), BF16),
            pltpu.VMEM((6, 48, 8, D), BF16),
            pltpu.VMEM((6, 384, D), BF16),
            pltpu.VMEM((6, 384, D), BF16),
            pltpu.VMEM((4, 256, D), BF16),
            pltpu.VMEM((4, 256, D), BF16),
            pltpu.VMEM((D, 3 * D), BF16),
            pltpu.VMEM((2, 2, 8, 9), jnp.int32),
            pltpu.SMEM((2, 2, 8, 9), jnp.int32),
            pltpu.VMEM((QUAD, KEYS), F32),
            pltpu.VMEM((QUAD, KEYS), F32),
            pltpu.VMEM((QUAD, KEYS), BF16),
            pltpu.VMEM((QUAD, KEYS), BF16),
            pltpu.VMEM((QUAD, 128), F32),
            pltpu.VMEM((QUAD, 128), F32),
            dma((3,)),
            dma,
            dma((STAGES, 4)),
            dma((STAGES, 2)),
            dma((STAGES, 2)),
            dma((2,)),
            dma((2,)),
            dma,
            dma,
            dma,
        ],
        compiler_params=pltpu.CompilerParams(
            collective_id=0, has_side_effects=True, vmem_limit_bytes=56 * 1024 * 1024
        ),
    )(tokens.reshape(2, GROUPS, 8, D), qkv_weight, neighbours)
    mixed = pl.pallas_call(
        mix_kernel,
        out_shape=jax.ShapeDtypeStruct((2, GROUPS, 8, D), BF16),
        in_specs=[pl.BlockSpec(memory_space=pltpu.VMEM)] * 2,
        out_specs=pl.BlockSpec(memory_space=pltpu.HBM),
        scratch_shapes=[
            pltpu.VMEM((GROUPS // MIX, 2, MIX, 8, D), BF16),
            dma((GROUPS // MIX,)),
        ],
        compiler_params=pltpu.CompilerParams(vmem_limit_bytes=32 * 1024 * 1024),
    )(attended, out_weight)
    return mixed.reshape(1024, D)


def solution(mesh):
    in_specs = (P(("rows", "cols"), None), P(), P(), P("rows", "cols", None))
    out_specs = P(("rows", "cols"), None)
    return jax.shard_map(
        per_device, mesh=mesh, in_specs=in_specs, out_specs=out_specs, check_vma=False
    )
```

```python
import functools

import jax
import jax.numpy as jnp
from jax import lax
from jax.experimental import pallas as pl
from jax.experimental.pallas import tpu as pltpu
from jax.sharding import PartitionSpec as P

MESH = pl.DeviceIdType.MESH
BF16 = jnp.bfloat16
F32 = jnp.float32
D = 1024
HEADS = 16
HEAD_DIM = 64
GROUPS = 64
TILES = 8
SCALE = HEAD_DIM**-0.5
STAGES = 6
COLS = 4
QUAD = 256
QUADS = HEADS // 4
KEYS = 576
MIX = 16


def kernel(
    tok, wqkv, nbr, out,
    src, win, keys, vals, quer, att, wqkv_v, nb_v, nb_s,
    score_a, score_b, prob_a, prob_b, share_a, share_b,
    load_sem, in_send, in_recv, halo_send, halo_recv, nb_send, nb_recv, nb_load, out_send, out_recv,
):
    scores, probs, shares = (score_a, score_b), (prob_a, prob_b), (share_a, share_b)
    row, col = lax.axis_index("rows"), lax.axis_index("cols")
    y, x_lo, core = row // 4, (row // 2) % 2, row % 2
    x_hi, z = col // 4, col % 4
    x = 2 * x_hi + x_lo
    g, t = 2 * y + core, 8 * x_lo + col
    has_up, has_down = g > 0, g < TILES - 1

    loads = [pltpu.make_async_copy(tok.at[r], src.at[pl.ds(1, GROUPS), r], load_sem.at[r]) for r in range(2)]
    wload = pltpu.make_async_copy(wqkv, wqkv_v, load_sem.at[2])
    for load in loads:
        load.start()
    wload.start()

    barrier = pltpu.get_barrier_semaphore()
    meets = core == x_lo

    def greet(i, carry):
        turn = i // 8
        other = jnp.where(turn == 0, x_lo, jnp.where(turn == 1, 2 + x_lo, 2 * core + 1 - x_lo))
        col2 = (col + i) % 8
        itself = jnp.logical_and(other == 2 * x_lo + core, col2 == col)

        @pl.when(jnp.logical_not(itself))
        def _():
            pl.semaphore_signal(barrier, inc=1, device_id=(4 * y + other, col2), device_id_type=MESH)

        return carry

    lax.fori_loop(0, 24, greet, 0)
    step_y = 2 * core - 1
    outer = jnp.logical_and(y + step_y >= 0, y + step_y < TILES // 2)

    @pl.when(outer)
    def _():
        pl.semaphore_signal(
            barrier, inc=1, device_id=(4 * (y + step_y) + 2 * x_lo + 1 - core, col), device_id_type=MESH
        )

    prob_b[...] = jnp.zeros_like(prob_b)
    share_b[...] = jnp.zeros_like(share_b)
    src[0] = jnp.zeros((2, 8, D), BF16)
    src[GROUPS + 1] = jnp.zeros((2, 8, D), BF16)

    @pl.when(jnp.logical_not(has_up))
    def _():
        for c in range(6):
            win[c, 0:8] = jnp.zeros((8, 8, D), BF16)

    @pl.when(jnp.logical_not(has_down))
    def _():
        for c in range(6):
            win[c, 40:48] = jnp.zeros((8, 8, D), BF16)

    for load in loads:
        load.wait()
    pl.semaphore_wait(barrier, 24 - jnp.where(meets, 1, 0) + jnp.where(outer, 1, 0))

    for e in range(2):
        there = 2 * col + e
        dest = (4 * y + 2 * x_hi + x_lo, there % 8)
        own = jnp.logical_and(dest[0] == row, dest[1] == col)

        @pl.when(own)
        def _(dest=dest):
            pltpu.make_async_copy(nbr, nb_v.at[core], nb_recv.at[core]).start()

        @pl.when(jnp.logical_not(own))
        def _(dest=dest, e=e):
            pltpu.make_async_remote_copy(
                nbr, nb_v.at[core], nb_send.at[e], nb_recv.at[core], device_id=dest, device_id_type=MESH
            ).start()

    at_row = 8 + 16 * core + 2 * col
    band = 2 * core + x_hi

    shift = jnp.where(t == 0, 1, 0)

    def place_of(k):
        return (k + shift) % 6

    def send_in(n, carry):
        k, s = n // 16, n % 16
        turn = (5 * s) % 16
        x2, z2 = (x + turn // 4) % 4, (z + turn) % 4
        col2 = 4 * (x2 // 2) + z2
        t2 = 8 * (x2 % 2) + col2
        c2 = (k + jnp.where(t2 == 0, 1, 0)) % 6
        source = src.at[4 * t2 + c2]
        target = win.at[c2, pl.ds(at_row, 2)]
        own = jnp.logical_and(s == 0, meets)

        @pl.when(own)
        def _():
            pltpu.make_async_copy(source, target, in_recv.at[k, band]).start()

        @pl.when(jnp.logical_not(own))
        def _():
            pltpu.make_async_remote_copy(
                source, target, in_send, in_recv.at[k, band],
                device_id=(4 * y + 2 * (x2 % 2) + x_lo, col2), device_id_type=MESH,
            ).start()

        return carry

    lax.fori_loop(0, 16 * STAGES, send_in, 0)

    def band_wait(k, b):
        part = win.at[0, pl.ds(8 + 8 * b, 8)]
        pltpu.make_async_copy(part, part, in_recv.at[k, b]).wait()

    def halo(k, down):
        c = place_of(k)
        g2 = g + 1 if down else g - 1
        source = win.at[c, pl.ds(32 if down else 8, 8)]
        target = win.at[c, pl.ds(0 if down else 40, 8)]
        way = 1 if down else 0
        return pltpu.make_async_remote_copy(
            source, target, halo_send.at[k, way], halo_recv.at[k, way],
            device_id=(4 * (g2 // 2) + 2 * x_lo + g2 % 2, col), device_id_type=MESH,
        )

    def arrive(k):
        band_wait(k, 0)

        @pl.when(has_up)
        def _():
            halo(k, False).start()

        band_wait(k, 3)

        @pl.when(has_down)
        def _():
            halo(k, True).start()

        band_wait(k, 1)
        band_wait(k, 2)

    def halo_wait(k):
        @pl.when(has_up)
        def _():
            halo(k, True).wait_recv()

        @pl.when(has_down)
        def _():
            halo(k, False).wait_recv()

    def project(x_in, store):
        kk = jnp.dot(x_in, wqkv_v[:, D : 2 * D], preferred_element_type=F32)
        vv = jnp.dot(x_in, wqkv_v[:, 2 * D :], preferred_element_type=F32)
        store(slice(None), kk.astype(BF16), vv.astype(BF16))

    def project_inner(k):
        c = place_of(k)

        def store(lanes, kk, vv):
            keys[c, 64:320, lanes] = kk
            vals[c, 64:320, lanes] = vv

        project(win[c, 8:40].reshape(256, D), store)

    def project_whole(k):
        c = place_of(k)

        def store(lanes, kk, vv):
            keys[c, :, lanes] = kk
            vals[c, :, lanes] = vv

        project(win[c].reshape(384, D), store)

    def project_halo(ks):
        places = [place_of(k) for k in ks]

        def store(lanes, kk, vv):
            for i, c in enumerate(places):
                keys[c, 0:64, lanes] = kk[128 * i : 128 * i + 64]
                keys[c, 320:384, lanes] = kk[128 * i + 64 : 128 * i + 128]
                vals[c, 0:64, lanes] = vv[128 * i : 128 * i + 64]
                vals[c, 320:384, lanes] = vv[128 * i + 64 : 128 * i + 128]

        parts = []
        for c in places:
            parts += [win[c, 0:8].reshape(64, D), win[c, 40:48].reshape(64, D)]
        project(jnp.concatenate(parts, axis=0), store)

    def project_queries(j):
        x_in = win[j + 1, 8:40].reshape(256, D)

        qq = jnp.dot(x_in, wqkv_v[:, :D], preferred_element_type=F32)
        quer[j] = (qq.astype(BF16) * SCALE).astype(BF16)

    lane_head = lax.broadcasted_iota(jnp.int32, (1, QUAD), 1) // HEAD_DIM

    key_at = lax.broadcasted_iota(jnp.int32, (1, KEYS), 1) // 64

    def attend(j, between):
        at_col = j
        if j == 0:
            at_col = j + shift
        if j == 3:
            at_col = j - jnp.where(t == 15, 1, 0)

        def key_rows(i):
            at_blk = i + jnp.where(jnp.logical_and(g == 0, i == 0), 1, 0)
            at_blk = at_blk - jnp.where(jnp.logical_and(g == TILES - 1, i == 3), 1, 0)
            return pl.ds(pl.multiple_of(64 * at_blk, 64), 192)

        def score(i, h):
            rows, lanes = key_rows(i), pl.ds(h * QUAD, QUAD)
            q4 = quer[j, pl.ds(pl.multiple_of(64 * i, 64), 64), lanes]
            stacked = jnp.concatenate(
                [jnp.where(lane_head == n, q4, jnp.zeros_like(q4)) for n in range(4)], axis=0
            )
            k4 = jnp.concatenate([keys[at_col + kc, rows, lanes] for kc in range(3)], axis=0)
            scores[h % 2][...] = lax.dot_general(
                stacked, k4, (((1,), (1,)), ((), ())), preferred_element_type=F32
            )

        def soften(bias, h):
            for r in range(0, QUAD, 32):
                s = scores[h % 2][r : r + 32, :] + bias
                p = jnp.exp(s - jnp.max(s, axis=1, keepdims=True))
                probs[h % 2][r : r + 32, :] = p.astype(BF16)
                share = 1.0 / jnp.sum(p, axis=1, keepdims=True)
                shares[h % 2][r : r + 32, :] = jnp.broadcast_to(share, (32, 128))

        def gather(i, h):
            rows, lanes = key_rows(i), pl.ds(h * QUAD, QUAD)
            v4 = jnp.concatenate([vals[at_col + kc, rows, lanes] for kc in range(3)], axis=0)
            r = jnp.dot(probs[h % 2][...], v4, preferred_element_type=F32)
            share = shares[h % 2][...]
            r = r * jnp.concatenate([share, share], axis=1)
            o = jnp.where(lane_head == 0, r[0:64], r[64:128])
            o = jnp.where(lane_head == 2, r[128:192], o)
            o = jnp.where(lane_head == 3, r[192:256], o)
            att[j, pl.ds(pl.multiple_of(64 * i, 64), 64), lanes] = o.astype(BF16)

        def block(n, carry):
            if between is not None:
                pl.when(n == 2)(between)
            i, before, after = turned(n), turned(jnp.maximum(n - 1, 0)), turned(jnp.minimum(n + 1, 3))
            bias = jnp.zeros((1, KEYS), F32)
            for kc in range(3):
                for kr in range(3):
                    entry = nb_s[i // 2, i % 2, 4 * (col % 2) + j, 3 * kr + kc]
                    here = jnp.where(entry >= 0, 0.0, -jnp.inf).astype(F32)
                    bias = jnp.where(key_at == 3 * kc + kr, here, bias)
            for h in range(QUADS):
                if h < QUADS - 1:
                    score(i, h + 1)
                else:
                    score(after, 0)
                if h > 0:
                    gather(i, h - 1)
                else:
                    gather(before, QUADS - 1)
                soften(bias, h)

            @pl.when(n > 0)
            def _():
                send_out(j, before)

            return carry

        score(turned(0), 0)
        lax.fori_loop(0, 4, block, 0)
        gather(turned(3), QUADS - 1)
        send_out(j, turned(3))

    def turned(n):
        return (n + 2 * core + x_hi) % 4

    def send_out(j, i):
        def send(s, carry):
            z2 = (z + s) % 4
            source = att.at[j, pl.ds(pl.multiple_of(64 * i + 16 * z2, 16), 16)]
            target = out.at[4 * t + j]
            own = jnp.logical_and(jnp.logical_and(s == 0, meets), i == 2 * core + x_hi)

            @pl.when(own)
            def _():
                pltpu.make_async_copy(source, target, out_recv).start()

            @pl.when(jnp.logical_not(own))
            def _():
                pltpu.make_async_remote_copy(
                    source, target, out_send, out_recv,
                    device_id=(4 * y + 2 * core + i // 2, 4 * (i % 2) + z2), device_id_type=MESH,
                ).start()

            return carry

        lax.fori_loop(0, 4, send, 0)

    def lists_in():
        for b in range(2):
            part = nb_v.at[b]
            pltpu.make_async_copy(part, part, nb_recv.at[b]).wait()
        down = pltpu.make_async_copy(nb_v, nb_s, nb_load)
        down.start()
        down.wait()

    wload.wait()
    arrive(0)
    project_inner(0)
    arrive(1)
    project_inner(1)
    project_queries(0)
    halo_wait(0)
    project_halo((0,))
    lists_in()
    arrive(2)
    project_inner(2)
    project_queries(1)
    halo_wait(1)
    halo_wait(2)
    project_halo((1, 2))
    for j in range(COLS):
        if j > 0:
            if j > 1:
                project_queries(j)
            halo_wait(j + 2)
            project_whole(j + 2)
        attend(j, functools.partial(arrive, j + 3) if j + 3 < STAGES else None)

    for e in range(2):
        there = 2 * col + e
        own = jnp.logical_and(4 * y + 2 * x_hi + x_lo == row, there % 8 == col)

        @pl.when(jnp.logical_not(own))
        def _(e=e):
            pltpu.make_async_copy(nbr, nbr, nb_send.at[e]).wait()

    for number, when in ((15, meets), (16, jnp.logical_not(meets))):

        @pl.when(when)
        def _(number=number):
            sent = win.at[:, pl.ds(0, 2 * number)]
            pltpu.make_async_copy(sent, sent, in_send).wait()
            back = att.at[:, pl.ds(0, 16 * number)]
            pltpu.make_async_copy(back, back, out_send).wait()

    for k in range(STAGES):

        @pl.when(has_up)
        def _(k=k):
            halo(k, False).wait_send()

        @pl.when(has_down)
        def _(k=k):
            halo(k, True).wait_send()

    pltpu.make_async_copy(out, out, out_recv).wait()


def mix_kernel(att, wout, out, mixed, out_sem):
    parts = GROUPS // MIX
    at = lambda n: pl.ds(n * MIX, MIX)
    stores = [pltpu.make_async_copy(mixed.at[n], out.at[:, at(n)], out_sem.at[n]) for n in range(parts)]
    for n in range(parts):
        x_in = att[at(n)].reshape(16 * MIX, D)
        mm = jnp.dot(x_in, wout[...], preferred_element_type=F32).astype(BF16)
        mm = mm.reshape(MIX, 2, 8, D)
        for r in range(2):
            mixed[n, r] = mm[:, r]
        stores[n].start()
    for store in stores:
        store.wait()


def per_device(tokens, qkv_weight, out_weight, neighbours):
    any_space = pl.BlockSpec(memory_space=pl.ANY)
    dma = pltpu.SemaphoreType.DMA
    attended = pl.pallas_call(
        kernel,
        out_shape=jax.ShapeDtypeStruct((GROUPS, 16, D), BF16),
        in_specs=[any_space] * 3,
        out_specs=any_space,
        scratch_shapes=[
            pltpu.VMEM((GROUPS + 2, 2, 8, D), BF16),
            pltpu.VMEM((6, 48, 8, D), BF16),
            pltpu.VMEM((6, 384, D), BF16),
            pltpu.VMEM((6, 384, D), BF16),
            pltpu.VMEM((4, 256, D), BF16),
            pltpu.VMEM((4, 256, D), BF16),
            pltpu.VMEM((D, 3 * D), BF16),
            pltpu.VMEM((2, 2, 8, 9), jnp.int32),
            pltpu.SMEM((2, 2, 8, 9), jnp.int32),
            pltpu.VMEM((QUAD, KEYS), F32),
            pltpu.VMEM((QUAD, KEYS), F32),
            pltpu.VMEM((QUAD, KEYS), BF16),
            pltpu.VMEM((QUAD, KEYS), BF16),
            pltpu.VMEM((QUAD, 128), F32),
            pltpu.VMEM((QUAD, 128), F32),
            dma((3,)),
            dma,
            dma((STAGES, 4)),
            dma((STAGES, 2)),
            dma((STAGES, 2)),
            dma((2,)),
            dma((2,)),
            dma,
            dma,
            dma,
        ],
        compiler_params=pltpu.CompilerParams(
            collective_id=0, has_side_effects=True, vmem_limit_bytes=56 * 1024 * 1024
        ),
    )(tokens.reshape(2, GROUPS, 8, D), qkv_weight, neighbours)
    mixed = pl.pallas_call(
        mix_kernel,
        out_shape=jax.ShapeDtypeStruct((2, GROUPS, 8, D), BF16),
        in_specs=[pl.BlockSpec(memory_space=pltpu.VMEM)] * 2,
        out_specs=pl.BlockSpec(memory_space=pltpu.HBM),
        scratch_shapes=[
            pltpu.VMEM((GROUPS // MIX, 2, MIX, 8, D), BF16),
            dma((GROUPS // MIX,)),
        ],
        compiler_params=pltpu.CompilerParams(vmem_limit_bytes=32 * 1024 * 1024),
    )(attended, out_weight)
    return mixed.reshape(1024, D)


def solution(mesh):
    in_specs = (P(("rows", "cols"), None), P(), P(), P("rows", "cols", None))
    out_specs = P(("rows", "cols"), None)
    return jax.shard_map(
        per_device, mesh=mesh, in_specs=in_specs, out_specs=out_specs, check_vma=False
    )
```

```python
import functools

import jax
import jax.numpy as jnp
from jax import lax
from jax.experimental import pallas as pl
from jax.experimental.pallas import tpu as pltpu
from jax.sharding import PartitionSpec as P

MESH = pl.DeviceIdType.MESH
BF16 = jnp.bfloat16
F32 = jnp.float32
D = 1024
HEADS = 16
HEAD_DIM = 64
GROUPS = 64
TILES = 8
SCALE = HEAD_DIM**-0.5
STAGES = 6
COLS = 4
QUAD = 256
QUADS = HEADS // 4
KEYS = 576
MIX = 16


def kernel(
    tok, wqkv, nbr, out,
    src, win, keys, vals, quer, att, wqkv_v, nb_v, nb_s,
    score_a, score_b, prob_a, prob_b, share_a, share_b,
    load_sem, in_send, in_recv, halo_send, halo_recv, nb_send, nb_recv, nb_load, out_send, out_recv,
):
    scores, probs, shares = (score_a, score_b), (prob_a, prob_b), (share_a, share_b)
    row, col = lax.axis_index("rows"), lax.axis_index("cols")
    y, x_lo, core = row // 4, (row // 2) % 2, row % 2
    x_hi, z = col // 4, col % 4
    x = 2 * x_hi + x_lo
    g, t = 2 * y + core, 8 * x_lo + col
    has_up, has_down = g > 0, g < TILES - 1

    loads = [pltpu.make_async_copy(tok.at[r], src.at[pl.ds(1, GROUPS), r], load_sem.at[r]) for r in range(2)]
    wload = pltpu.make_async_copy(wqkv, wqkv_v, load_sem.at[2])
    for load in loads:
        load.start()
    wload.start()

    barrier = pltpu.get_barrier_semaphore()
    meets = core == x_lo

    def greet(i, carry):
        turn = i // 8
        other = jnp.where(turn == 0, x_lo, jnp.where(turn == 1, 2 + x_lo, 2 * core + 1 - x_lo))
        col2 = (col + i) % 8
        itself = jnp.logical_and(other == 2 * x_lo + core, col2 == col)

        @pl.when(jnp.logical_not(itself))
        def _():
            pl.semaphore_signal(barrier, inc=1, device_id=(4 * y + other, col2), device_id_type=MESH)

        return carry

    lax.fori_loop(0, 24, greet, 0)
    step_y = 2 * core - 1
    outer = jnp.logical_and(y + step_y >= 0, y + step_y < TILES // 2)

    @pl.when(outer)
    def _():
        pl.semaphore_signal(
            barrier, inc=1, device_id=(4 * (y + step_y) + 2 * x_lo + 1 - core, col), device_id_type=MESH
        )

    prob_b[...] = jnp.zeros_like(prob_b)
    share_b[...] = jnp.zeros_like(share_b)
    src[0] = jnp.zeros((2, 8, D), BF16)
    src[GROUPS + 1] = jnp.zeros((2, 8, D), BF16)

    @pl.when(jnp.logical_not(has_up))
    def _():
        for c in range(6):
            win[c, 0:8] = jnp.zeros((8, 8, D), BF16)

    @pl.when(jnp.logical_not(has_down))
    def _():
        for c in range(6):
            win[c, 40:48] = jnp.zeros((8, 8, D), BF16)

    for load in loads:
        load.wait()
    pl.semaphore_wait(barrier, 24 - jnp.where(meets, 1, 0) + jnp.where(outer, 1, 0))

    at_row = 8 + 16 * core + 2 * col
    band = 2 * core + x_hi

    shift = jnp.where(t == 0, 1, 0)

    def place_of(k):
        return (k + shift) % 6

    def send_in(n, carry):
        k, s = n // 16, n % 16
        turn = (5 * s) % 16
        x2, z2 = (x + turn // 4) % 4, (z + turn) % 4
        col2 = 4 * (x2 // 2) + z2
        t2 = 8 * (x2 % 2) + col2
        c2 = (k + jnp.where(t2 == 0, 1, 0)) % 6
        source = src.at[4 * t2 + c2]
        target = win.at[c2, pl.ds(at_row, 2)]
        own = jnp.logical_and(s == 0, meets)

        @pl.when(own)
        def _():
            pltpu.make_async_copy(source, target, in_recv.at[k, band]).start()

        @pl.when(jnp.logical_not(own))
        def _():
            pltpu.make_async_remote_copy(
                source, target, in_send, in_recv.at[k, band],
                device_id=(4 * y + 2 * (x2 % 2) + x_lo, col2), device_id_type=MESH,
            ).start()

        return carry

    lax.fori_loop(0, 16, send_in, 0)

    for e in range(2):
        there = 2 * col + e
        dest = (4 * y + 2 * x_hi + x_lo, there % 8)
        own = jnp.logical_and(dest[0] == row, dest[1] == col)

        @pl.when(own)
        def _(dest=dest):
            pltpu.make_async_copy(nbr, nb_v.at[core], nb_recv.at[core]).start()

        @pl.when(jnp.logical_not(own))
        def _(dest=dest, e=e):
            pltpu.make_async_remote_copy(
                nbr, nb_v.at[core], nb_send.at[e], nb_recv.at[core], device_id=dest, device_id_type=MESH
            ).start()

    lax.fori_loop(16, 16 * STAGES, send_in, 0)

    def band_wait(k, b):
        part = win.at[0, pl.ds(8 + 8 * b, 8)]
        pltpu.make_async_copy(part, part, in_recv.at[k, b]).wait()

    def halo(k, down):
        c = place_of(k)
        g2 = g + 1 if down else g - 1
        source = win.at[c, pl.ds(32 if down else 8, 8)]
        target = win.at[c, pl.ds(0 if down else 40, 8)]
        way = 1 if down else 0
        return pltpu.make_async_remote_copy(
            source, target, halo_send.at[k, way], halo_recv.at[k, way],
            device_id=(4 * (g2 // 2) + 2 * x_lo + g2 % 2, col), device_id_type=MESH,
        )

    def arrive(k):
        band_wait(k, 0)

        @pl.when(has_up)
        def _():
            halo(k, False).start()

        band_wait(k, 3)

        @pl.when(has_down)
        def _():
            halo(k, True).start()

        band_wait(k, 1)
        band_wait(k, 2)

    def halo_wait(k):
        @pl.when(has_up)
        def _():
            halo(k, True).wait_recv()

        @pl.when(has_down)
        def _():
            halo(k, False).wait_recv()

    def project(x_in, store):
        kk = jnp.dot(x_in, wqkv_v[:, D : 2 * D], preferred_element_type=F32)
        vv = jnp.dot(x_in, wqkv_v[:, 2 * D :], preferred_element_type=F32)
        store(slice(None), kk.astype(BF16), vv.astype(BF16))

    def project_inner(k):
        c = place_of(k)

        def store(lanes, kk, vv):
            keys[c, 64:320, lanes] = kk
            vals[c, 64:320, lanes] = vv

        project(win[c, 8:40].reshape(256, D), store)

    def project_whole(k):
        c = place_of(k)

        def store(lanes, kk, vv):
            keys[c, :, lanes] = kk
            vals[c, :, lanes] = vv

        project(win[c].reshape(384, D), store)

    def project_halo(ks):
        places = [place_of(k) for k in ks]

        def store(lanes, kk, vv):
            for i, c in enumerate(places):
                keys[c, 0:64, lanes] = kk[128 * i : 128 * i + 64]
                keys[c, 320:384, lanes] = kk[128 * i + 64 : 128 * i + 128]
                vals[c, 0:64, lanes] = vv[128 * i : 128 * i + 64]
                vals[c, 320:384, lanes] = vv[128 * i + 64 : 128 * i + 128]

        parts = []
        for c in places:
            parts += [win[c, 0:8].reshape(64, D), win[c, 40:48].reshape(64, D)]
        project(jnp.concatenate(parts, axis=0), store)

    def project_queries(j):
        x_in = win[j + 1, 8:40].reshape(256, D)

        qq = jnp.dot(x_in, wqkv_v[:, :D], preferred_element_type=F32)
        quer[j] = (qq.astype(BF16) * SCALE).astype(BF16)

    lane_head = lax.broadcasted_iota(jnp.int32, (1, QUAD), 1) // HEAD_DIM

    key_at = lax.broadcasted_iota(jnp.int32, (1, KEYS), 1) // 64

    def attend(j, between):
        at_col = j
        if j == 0:
            at_col = j + shift
        if j == 3:
            at_col = j - jnp.where(t == 15, 1, 0)

        def key_rows(i):
            at_blk = i + jnp.where(jnp.logical_and(g == 0, i == 0), 1, 0)
            at_blk = at_blk - jnp.where(jnp.logical_and(g == TILES - 1, i == 3), 1, 0)
            return pl.ds(pl.multiple_of(64 * at_blk, 64), 192)

        def score(i, h):
            rows, lanes = key_rows(i), pl.ds(h * QUAD, QUAD)
            q4 = quer[j, pl.ds(pl.multiple_of(64 * i, 64), 64), lanes]
            stacked = jnp.concatenate(
                [jnp.where(lane_head == n, q4, jnp.zeros_like(q4)) for n in range(4)], axis=0
            )
            k4 = jnp.concatenate([keys[at_col + kc, rows, lanes] for kc in range(3)], axis=0)
            scores[h % 2][...] = lax.dot_general(
                stacked, k4, (((1,), (1,)), ((), ())), preferred_element_type=F32
            )

        def soften(bias, h):
            for r in range(0, QUAD, 32):
                s = scores[h % 2][r : r + 32, :] + bias
                p = jnp.exp(s - jnp.max(s, axis=1, keepdims=True))
                probs[h % 2][r : r + 32, :] = p.astype(BF16)
                share = 1.0 / jnp.sum(p, axis=1, keepdims=True)
                shares[h % 2][r : r + 32, :] = jnp.broadcast_to(share, (32, 128))

        def gather(i, h):
            rows, lanes = key_rows(i), pl.ds(h * QUAD, QUAD)
            v4 = jnp.concatenate([vals[at_col + kc, rows, lanes] for kc in range(3)], axis=0)
            r = jnp.dot(probs[h % 2][...], v4, preferred_element_type=F32)
            share = shares[h % 2][...]
            r = r * jnp.concatenate([share, share], axis=1)
            o = jnp.where(lane_head == 0, r[0:64], r[64:128])
            o = jnp.where(lane_head == 2, r[128:192], o)
            o = jnp.where(lane_head == 3, r[192:256], o)
            att[j, pl.ds(pl.multiple_of(64 * i, 64), 64), lanes] = o.astype(BF16)

        def block(n, carry):
            if between is not None:
                pl.when(n == 2)(between)
            i, before, after = turned(n), turned(jnp.maximum(n - 1, 0)), turned(jnp.minimum(n + 1, 3))
            bias = jnp.zeros((1, KEYS), F32)
            for kc in range(3):
                for kr in range(3):
                    entry = nb_s[i // 2, i % 2, 4 * (col % 2) + j, 3 * kr + kc]
                    here = jnp.where(entry >= 0, 0.0, -jnp.inf).astype(F32)
                    bias = jnp.where(key_at == 3 * kc + kr, here, bias)
            for h in range(QUADS):
                if h < QUADS - 1:
                    score(i, h + 1)
                else:
                    score(after, 0)
                if h > 0:
                    gather(i, h - 1)
                else:
                    gather(before, QUADS - 1)
                soften(bias, h)

            @pl.when(n > 0)
            def _():
                send_out(j, before)

            return carry

        score(turned(0), 0)
        lax.fori_loop(0, 4, block, 0)
        gather(turned(3), QUADS - 1)
        send_out(j, turned(3))

    def turned(n):
        return (n + 2 * core + x_hi) % 4

    def send_out(j, i):
        def send(s, carry):
            z2 = (z + s) % 4
            source = att.at[j, pl.ds(pl.multiple_of(64 * i + 16 * z2, 16), 16)]
            target = out.at[4 * t + j]
            own = jnp.logical_and(jnp.logical_and(s == 0, meets), i == 2 * core + x_hi)

            @pl.when(own)
            def _():
                pltpu.make_async_copy(source, target, out_recv).start()

            @pl.when(jnp.logical_not(own))
            def _():
                pltpu.make_async_remote_copy(
                    source, target, out_send, out_recv,
                    device_id=(4 * y + 2 * core + i // 2, 4 * (i % 2) + z2), device_id_type=MESH,
                ).start()

            return carry

        lax.fori_loop(0, 4, send, 0)

    def lists_in():
        for b in range(2):
            part = nb_v.at[b]
            pltpu.make_async_copy(part, part, nb_recv.at[b]).wait()
        down = pltpu.make_async_copy(nb_v, nb_s, nb_load)
        down.start()
        down.wait()

    wload.wait()
    arrive(0)
    project_inner(0)
    arrive(1)
    project_inner(1)
    project_queries(0)
    halo_wait(0)
    project_halo((0,))
    lists_in()
    arrive(2)
    project_inner(2)
    project_queries(1)
    halo_wait(1)
    halo_wait(2)
    project_halo((1, 2))
    for j in range(COLS):
        if j > 0:
            if j > 1:
                project_queries(j)
            halo_wait(j + 2)
            project_whole(j + 2)
        attend(j, functools.partial(arrive, j + 3) if j + 3 < STAGES else None)

    for e in range(2):
        there = 2 * col + e
        own = jnp.logical_and(4 * y + 2 * x_hi + x_lo == row, there % 8 == col)

        @pl.when(jnp.logical_not(own))
        def _(e=e):
            pltpu.make_async_copy(nbr, nbr, nb_send.at[e]).wait()

    for number, when in ((15, meets), (16, jnp.logical_not(meets))):

        @pl.when(when)
        def _(number=number):
            sent = win.at[:, pl.ds(0, 2 * number)]
            pltpu.make_async_copy(sent, sent, in_send).wait()
            back = att.at[:, pl.ds(0, 16 * number)]
            pltpu.make_async_copy(back, back, out_send).wait()

    for k in range(STAGES):

        @pl.when(has_up)
        def _(k=k):
            halo(k, False).wait_send()

        @pl.when(has_down)
        def _(k=k):
            halo(k, True).wait_send()

    pltpu.make_async_copy(out, out, out_recv).wait()


def mix_kernel(att, wout, out, mixed, out_sem):
    parts = GROUPS // MIX
    at = lambda n: pl.ds(n * MIX, MIX)
    stores = [pltpu.make_async_copy(mixed.at[n], out.at[:, at(n)], out_sem.at[n]) for n in range(parts)]
    for n in range(parts):
        x_in = att[at(n)].reshape(16 * MIX, D)
        mm = jnp.dot(x_in, wout[...], preferred_element_type=F32).astype(BF16)
        mm = mm.reshape(MIX, 2, 8, D)
        for r in range(2):
            mixed[n, r] = mm[:, r]
        stores[n].start()
    for store in stores:
        store.wait()


def per_device(tokens, qkv_weight, out_weight, neighbours):
    any_space = pl.BlockSpec(memory_space=pl.ANY)
    dma = pltpu.SemaphoreType.DMA
    attended = pl.pallas_call(
        kernel,
        out_shape=jax.ShapeDtypeStruct((GROUPS, 16, D), BF16),
        in_specs=[any_space] * 3,
        out_specs=any_space,
        scratch_shapes=[
            pltpu.VMEM((GROUPS + 2, 2, 8, D), BF16),
            pltpu.VMEM((6, 48, 8, D), BF16),
            pltpu.VMEM((6, 384, D), BF16),
            pltpu.VMEM((6, 384, D), BF16),
            pltpu.VMEM((4, 256, D), BF16),
            pltpu.VMEM((4, 256, D), BF16),
            pltpu.VMEM((D, 3 * D), BF16),
            pltpu.VMEM((2, 2, 8, 9), jnp.int32),
            pltpu.SMEM((2, 2, 8, 9), jnp.int32),
            pltpu.VMEM((QUAD, KEYS), F32),
            pltpu.VMEM((QUAD, KEYS), F32),
            pltpu.VMEM((QUAD, KEYS), BF16),
            pltpu.VMEM((QUAD, KEYS), BF16),
            pltpu.VMEM((QUAD, 128), F32),
            pltpu.VMEM((QUAD, 128), F32),
            dma((3,)),
            dma,
            dma((STAGES, 4)),
            dma((STAGES, 2)),
            dma((STAGES, 2)),
            dma((2,)),
            dma((2,)),
            dma,
            dma,
            dma,
        ],
        compiler_params=pltpu.CompilerParams(
            collective_id=0, has_side_effects=True, vmem_limit_bytes=56 * 1024 * 1024
        ),
    )(tokens.reshape(2, GROUPS, 8, D), qkv_weight, neighbours)
    mixed = pl.pallas_call(
        mix_kernel,
        out_shape=jax.ShapeDtypeStruct((2, GROUPS, 8, D), BF16),
        in_specs=[pl.BlockSpec(memory_space=pltpu.VMEM)] * 2,
        out_specs=pl.BlockSpec(memory_space=pltpu.HBM),
        scratch_shapes=[
            pltpu.VMEM((GROUPS // MIX, 2, MIX, 8, D), BF16),
            dma((GROUPS // MIX,)),
        ],
        compiler_params=pltpu.CompilerParams(vmem_limit_bytes=32 * 1024 * 1024),
    )(attended, out_weight)
    return mixed.reshape(1024, D)


def solution(mesh):
    in_specs = (P(("rows", "cols"), None), P(), P(), P("rows", "cols", None))
    out_specs = P(("rows", "cols"), None)
    return jax.shard_map(
        per_device, mesh=mesh, in_specs=in_specs, out_specs=out_specs, check_vma=False
    )
```
